256 devices in a mesh: tile: 32 (over y, z), obs: 4 (over x), mem: 2 (over core).
Axes of the slice: x: 4, y: 4, z: 8, core: 2. Of those that a mesh axis runs over, the one named last changes fastest.
Arguments:
- ensemble: float32 [80, 1024, 256], P('mem', ('tile', 'obs')), may hold values from -6 to 6
- obs_cell: int32 [4, 2048], P('obs', 'tile'), may hold values from 0 to 262143
- obs_value: float32 [4, 2048], P('obs', 'tile'), may hold values from -8 to 8
- obs_var: float32 [4, 2048], P('obs', 'tile'), may hold values from 0.5 to 8
Outputs:
- analysis: float32 [80, 1024, 256], P('mem', ('tile', 'obs'))
The draws below stay inside these ranges and needn't reach their ends.
Inputs may be any that keep to these rules, and one draw needn't show every extreme that they name: `obs_cell`: observation cells are grid cells of the whole state.
All inputs are finite; a program needn't handle non-finite values.
Results may differ from the reference program's by a relative error of at most 0.0003.
Values sent between devices are 32-bit elements; how exact they have to be, the bound alone decides.
No kernel may reach another device: no remote copies, remote signals or barrier semaphores. Data moves between devices by JAX's collectives and lax.ppermute only.
A program may use at most 64 MiB of HBM per device.

```python
import math
import jax
import jax.numpy as jnp
from jax import lax

M = 80
P_SIZE = 256
NT = 1024
NOB = 2048
NB = 4
REACH = 512


def set_ends(values, own_key, least, high):
    extent = values.shape
    spot = [jax.random.randint(jax.random.fold_in(own_key, axis), (), 0, extent[axis]) for axis in range(len(extent))]
    values = values.at[tuple(spot)].set(least)
    longest = extent.index(max(extent))
    spot[longest] = (spot[longest] + 1) % extent[longest]
    return values.at[tuple(spot)].set(high)


def block_levels(key, shape, cuts, low, largest):
    factor_of, own = 1.0, jax.random.fold_in(key, 6)
    for axis_at, parts in cuts:
        steps = jnp.exp(jax.random.uniform(jax.random.fold_in(own, axis_at), (parts,), jnp.float32, low / len(cuts), largest / len(cuts)))
        factor_of = factor_of * jnp.repeat(steps, shape[axis_at] // parts).reshape([-1 if axis == axis_at else 1 for axis in range(len(shape))])
    return factor_of


def bell_draw(key, dims, width, bound, split=(), kind=jnp.bfloat16):
    factor_of = block_levels(key, dims, split, -0.22, 0.18) if split else 1.0
    values = jax.random.normal(key, dims, jnp.float32) * width * factor_of
    return jnp.minimum(jnp.maximum(values, -bound), bound).astype(kind)


def setup_inputs(seed: int = 0) -> dict:
    splits = jax.random.split(jax.random.key(seed), 5)
    return {
        "ensemble": bell_draw(splits[0], (M, NT, P_SIZE), 1.0, 6.0, ((0, 2), (1, 128)), jnp.float32),
        "obs_cell": set_ends(jax.random.randint(splits[1], (NB, NOB), 0, NT * P_SIZE), jax.random.fold_in(splits[1], 1), 0, (NT * P_SIZE) - 1).astype(jnp.int32),
        "obs_value": bell_draw(splits[2], (NB, NOB), 1.5, 8.0, ((0, 4), (1, 32)), jnp.float32),
        "obs_var": jnp.clip(jnp.exp(math.log(8.0) - 2.7725887 * jax.random.uniform(splits[3], (NB, NOB), jnp.float32) ** block_levels(splits[3], (NB, NOB), ((0, 4), (1, 32)), -0.2, 0.2)), 0.5, 8.0),
    }


def taper(dist, reach):
    z = dist / reach
    inner = (((-0.25 * z + 0.5) * z + 0.625) * z - 5.0 / 3.0) * z * z + 1.0
    outer = ((((z / 12.0 - 0.5) * z + 0.625) * z + 5.0 / 3.0) * z - 5.0) * z + 4.0 - 2.0 / (3.0 * jnp.maximum(z, 1.0))
    return jnp.where(z <= 1.0, inner, jnp.where(z < 2.0, outer, jnp.zeros_like(z)))

def cycle_weight(tile_ids, obs_tiles, total):
    delta = jnp.abs(tile_ids[:, None] - obs_tiles[None, :]) % total
    dist = jnp.minimum(delta, total - delta).astype(jnp.float32)
    return taper(dist, jnp.float32(REACH))

def update_tile(anom, centre, weights, factors, spread):
    weight_a, weight_d, pa = factors
    scaled = pa * (weights * weight_a)[None, :]
    gram = jnp.einsum('mj,nj->mn', scaled, pa, precision=lax.Precision.HIGHEST)
    shift = jnp.dot(pa, weights * weight_d, precision=lax.Precision.HIGHEST)
    new_centre = centre + jnp.dot(shift, anom, precision=lax.Precision.HIGHEST) / spread
    return new_centre[None, :] + anom - jnp.dot(gram, anom, precision=lax.Precision.HIGHEST) / spread

def reference(ensemble, obs_cell, obs_value, obs_var):
    state = ensemble
    spread = jnp.float32(M - 1)
    tile_ids = jnp.arange(NT, dtype=jnp.int32)
    for batch in range(NB):
        cells = obs_cell[batch]
        flat = state.reshape(M, NT * P_SIZE)
        prior = jnp.take(flat, cells, axis=1)
        pmean = lax.optimization_barrier(jnp.mean(prior, axis=0))
        pa = prior - pmean[None, :]
        total_var = lax.optimization_barrier(jnp.sum(pa * pa, axis=0)) / spread + obs_var[batch]
        alpha = 1.0 / (1.0 + jnp.sqrt(obs_var[batch] / total_var))
        weight_a = alpha / total_var
        weight_d = (obs_value[batch] - pmean) / total_var
        obs_tiles = cells // P_SIZE
        centre = lax.optimization_barrier(jnp.mean(state, axis=0))
        anom = state - centre[None]

        def per_tile(item):
            tile_one, anom_one, centre_one = item
            weights = cycle_weight(tile_one[None], obs_tiles, NT)[0]
            return update_tile(anom_one, centre_one, weights, (weight_a, weight_d, pa), spread)
        updated = lax.map(per_tile, (tile_ids, jnp.transpose(anom, (1, 0, 2)), centre))
        state = jnp.transpose(updated, (1, 0, 2))
    return state
```

```python
import functools

import jax
import jax.numpy as jnp
from jax import lax
from jax.experimental import pallas as pl
from jax.experimental.pallas import tpu as pltpu
from jax.sharding import PartitionSpec as P

HI = lax.Precision.HIGHEST
LANES = 128
VALUE, VAR, TILE = 0, 1, 2
MIB = 1024 * 1024


def taper(tile_a, tile_b, total):
    delta = jnp.abs(tile_a - tile_b)
    z = jnp.minimum(delta, total - delta) * (2.0 / total)
    return (((-0.25 * z + 0.5) * z + 0.625) * z - 5.0 / 3.0) * (z * z) + 1.0


def nt_dot(a, b):
    return lax.dot_general(
        a, b, (((1,), (1,)), ((), ())), precision=HI, preferred_element_type=jnp.float32
    )


def nn_dot(a, b):
    return jnp.dot(a, b, precision=HI, preferred_element_type=jnp.float32)


def pick_kernel(n_src, m_dev, tpd, points, info, idx, *refs):
    chunks, (out, cols) = refs[: 2 * n_src], refs[2 * n_src :]
    core = info[1]
    members = 2 * m_dev
    cells = tpd * points
    for src in range(n_src):
        own, other = chunks[src], chunks[n_src + src]
        for tile in range(tpd):
            for part in range(points // LANES):
                rows = pl.ds(part * m_dev * tpd + tile, m_dev, stride=tpd)
                a, b = own[rows, :], other[rows, :]
                block = jnp.concatenate(
                    [
                        jnp.where(core == 0, a, b),
                        jnp.where(core == 0, b, a),
                        jnp.zeros((LANES - members, LANES), jnp.float32),
                    ],
                    axis=0,
                )
                start = src * cells + tile * points + part * LANES
                cols[pl.ds(start, LANES), :] = block.T
    cols[pl.ds(n_src * cells, 8), :] = jnp.zeros((8, LANES), jnp.float32)

    def body(step, carry):
        base = pl.multiple_of(step * 16, 16)
        for row in range(16):
            out[pl.ds(base + row, 1), :] = cols[pl.ds(idx[base + row], 1), :]
        return carry

    lax.fori_loop(0, out.shape[0] // 16, body, 0)


def weights(block, members):
    rows = lax.broadcasted_iota(jnp.int32, block.shape, 0)
    real = rows < members
    mean = jnp.sum(jnp.where(real, block, 0.0), axis=0, keepdims=True) / members
    pa = jnp.where(real, block - mean, 0.0)
    value = block[members + VALUE : members + VALUE + 1]
    var = block[members + VAR : members + VAR + 1]
    tiles = block[members + TILE : members + TILE + 1]
    total_var = jnp.sum(pa * pa, axis=0, keepdims=True) / (members - 1) + var
    alpha = 1.0 / (1.0 + jnp.sqrt(var / total_var))
    weight_a = alpha / total_var
    weight_d = (value - mean) / total_var
    left = jnp.where(real, (weight_d - weight_a * pa) / (members - 1), 0.0)
    return pa, left, tiles


def update_rows(rows_x, pa, left, tiles, own_tiles, total):
    s = nn_dot(rows_x, pa)
    return nt_dot(taper(own_tiles, tiles, total) * s, left)


def next_kernel(members, total, own4, oth4, xt_ref, q_out, pa_out, left_out, tile_out):
    n_block, height, width = own4.shape
    xt = xt_ref[...]
    rows_x = xt[:, :height]
    own_tiles = xt[:, members + TILE : members + TILE + 1]
    acc = jnp.zeros(rows_x.shape, jnp.float32)
    for at in range(2 * n_block):
        block = (own4 if at < n_block else oth4)[at % n_block]
        pa, left, tiles = weights(block, members)
        acc += update_rows(rows_x, pa, left, tiles, own_tiles, total)
        cols = pl.ds(at * width, width)
        pa_out[:, cols] = pa
        left_out[:, cols] = left
        tile_out[:, cols] = tiles
    pad = jnp.zeros((rows_x.shape[0], LANES - height), jnp.float32)
    new = jnp.concatenate([rows_x + acc, pad], axis=1)
    q_out[...] = new.T[:height]


def state_part(members, total, tpd, info, pa_ref, left_ref, tile_ref, own, other, new):
    m_dev = members // 2
    height, n_obs = pa_ref.shape
    width = 256
    first, core = info[0], info[1]
    start = pl.multiple_of(core * m_dev, 8)
    gram = jnp.zeros((tpd * m_dev, height), jnp.float32)
    for at in range(n_obs // width):
        cols = pl.ds(at * width, width)
        left = left_ref[pl.ds(start, m_dev), cols]
        scaled = jnp.concatenate(
            [
                left * taper((first + tile).astype(jnp.float32), tile_ref[:, cols], total)
                for tile in range(tpd)
            ],
            axis=0,
        )
        gram += nt_dot(scaled, pa_ref[:, cols])
    for tile in range(tpd):
        for part in range(own.shape[0] // (m_dev * tpd)):
            rows = pl.ds(part * m_dev * tpd + tile, m_dev, stride=tpd)
            a, b = own[rows, :], other[rows, :]
            whole = jnp.concatenate(
                [jnp.where(core == 0, a, b), jnp.where(core == 0, b, a)], axis=0
            )
            one = gram[tile * m_dev : (tile + 1) * m_dev, :members]
            new[rows, :] = a + nn_dot(one, whole)


def later_kernel(members, total, tpd, info, pa_ref, left_ref, tile_ref, own, other, *refs):
    n_later = (len(refs) - 1) // 2
    xts, outs, new = refs[:n_later], refs[n_later : 2 * n_later], refs[-1]
    height, n_obs = pa_ref.shape
    width = 256
    for xt_ref, out in zip(xts, outs):
        xt = xt_ref[...]
        rows_x = xt[:, :height]
        own_tiles = xt[:, members + TILE : members + TILE + 1]
        acc = jnp.zeros(rows_x.shape, jnp.float32)
        for at in range(n_obs // width):
            cols = pl.ds(at * width, width)
            acc += update_rows(
                rows_x, pa_ref[:, cols], left_ref[:, cols], tile_ref[:, cols], own_tiles, total
            )
        pad = jnp.zeros((rows_x.shape[0], LANES - height), jnp.float32)
        out[...] = jnp.concatenate([rows_x + acc, pad], axis=1)
    state_part(members, total, tpd, info, pa_ref, left_ref, tile_ref, own, other, new)


def last_kernel(members, total, tpd, info, own4, oth4, own, other, new, pa_s, left_s, tile_s):
    n_block, _, width = own4.shape
    for at in range(2 * n_block):
        block = (own4 if at < n_block else oth4)[at % n_block]
        pa, left, tiles = weights(block, members)
        cols = pl.ds(at * width, width)
        pa_s[:, cols] = pa
        left_s[:, cols] = left
        tile_s[:, cols] = tiles
    state_part(members, total, tpd, info, pa_s, left_s, tile_s, own, other, new)


def vmem(n):
    return [pl.BlockSpec(memory_space=pltpu.VMEM)] * n


def smem(n):
    return [pl.BlockSpec(memory_space=pltpu.SMEM)] * n


def f32(*shape):
    return jax.ShapeDtypeStruct(shape, jnp.float32)


def ring(n, shift):
    return [(i, (i + shift) % n) for i in range(n)]


def per_device(ensemble, obs_cell, obs_value, obs_var):
    m_dev, tpd, points = ensemble.shape
    n_tile = lax.axis_size("tile")
    n_obs = lax.axis_size("obs")
    members = 2 * m_dev
    per_dev = obs_cell.shape[1]
    half = per_dev // 2
    part = half // n_obs
    batch_obs = per_dev * n_tile
    width = part * n_tile
    height = members + 8
    total = tpd * n_tile * n_obs
    slab_cells = tpd * points
    tile_at, obs_at, core = (lax.axis_index(a) for a in ("tile", "obs", "mem"))
    first_tile = (tile_at * n_obs + obs_at) * tpd
    info = jnp.stack([first_tile, core]).astype(jnp.int32)
    params = pltpu.CompilerParams(vmem_limit_bytes=40 * MIB)
    swap = functools.partial(lax.ppermute, axis_name="mem", perm=[(0, 1), (1, 0)])

    def shifted(x):
        return [x] + [lax.ppermute(x, "obs", ring(n_obs, k)) for k in range(1, n_obs)]

    state = jnp.transpose(ensemble.reshape(m_dev * tpd, points // LANES, LANES), (1, 0, 2))
    state = state.reshape(-1, LANES)
    chunks = shifted(state)
    others = [swap(chunk) for chunk in chunks]

    cells = obs_cell.astype(jnp.float32)
    sent = jnp.broadcast_to(jnp.concatenate([cells, cells], axis=1)[None], (n_tile, 1, 2 * per_dev))
    lists = lax.all_to_all(sent, "tile", 0, 0)
    mine = lax.dynamic_slice(lists, (0, 0, core * half), (n_tile, 1, half))
    mine = mine.reshape(n_tile * half).astype(jnp.int32)
    slab = mine // slab_cells
    source = (obs_at - slab % n_obs + n_obs) % n_obs
    idx = jnp.where(
        slab // n_obs == tile_at, source * slab_cells + mine % slab_cells, n_obs * slab_cells
    )

    picked = pl.pallas_call(
        functools.partial(pick_kernel, n_obs, m_dev, tpd, points),
        out_shape=f32(n_tile * half, LANES),
        in_specs=smem(2) + vmem(2 * n_obs),
        out_specs=pl.BlockSpec(memory_space=pltpu.VMEM),
        scratch_shapes=[pltpu.VMEM((n_obs * slab_cells + 8, LANES), jnp.float32)],
        compiler_params=params,
        name="pick",
    )(info, idx, *chunks, *others)

    parts = lax.all_to_all(picked.reshape(n_tile, half, LANES), "tile", 0, 0)
    lane = lax.broadcasted_iota(jnp.int32, (half, LANES), 1)

    def own_half(x):
        return lax.dynamic_slice(x, (0, core * half), (1, half)).reshape(half, 1)

    rows = jnp.sum(parts, axis=0)
    rows = jnp.where(lane == members + VALUE, own_half(obs_value), rows)
    rows = jnp.where(lane == members + VAR, own_half(obs_var), rows)
    rows = jnp.where(lane == members + TILE, own_half((obs_cell // points).astype(jnp.float32)), rows)
    sent = jnp.broadcast_to(rows.reshape(1, n_obs, part, LANES), (n_tile, n_obs, part, LANES))
    got = lax.all_to_all(sent.reshape(n_tile * n_obs, part, LANES), ("tile", "obs"), 0, 0)
    got = got.reshape(n_tile, n_obs, part, LANES)
    xts = [got[:, b].reshape(width, LANES) for b in range(n_obs)]

    other = others[0]
    q = xts[0].T[:height]
    xts = xts[1:]
    columns = batch_obs
    for batch in range(n_obs):
        own4 = jnp.stack(shifted(q))
        oth4 = swap(own4)
        if batch == n_obs - 1:
            state = pl.pallas_call(
                functools.partial(last_kernel, members, total, tpd),
                out_shape=f32(*state.shape),
                in_specs=smem(1) + vmem(4),
                out_specs=pl.BlockSpec(memory_space=pltpu.VMEM),
                scratch_shapes=[
                    pltpu.VMEM((height, columns), jnp.float32),
                    pltpu.VMEM((height, columns), jnp.float32),
                    pltpu.VMEM((1, columns), jnp.float32),
                ],
                compiler_params=params,
                name="last",
            )(info, own4, oth4, state, other)
            break
        q, pa, left, tiles = pl.pallas_call(
            functools.partial(next_kernel, members, total),
            out_shape=[
                f32(height, width),
                f32(height, columns),
                f32(height, columns),
                f32(1, columns),
            ],
            in_specs=vmem(3),
            out_specs=vmem(4),
            compiler_params=params,
            name=f"next{batch}",
        )(own4, oth4, xts[0])
        xts = xts[1:]
        *xts, state = pl.pallas_call(
            functools.partial(later_kernel, members, total, tpd),
            out_shape=[f32(width, LANES)] * len(xts) + [f32(*state.shape)],
            in_specs=smem(1) + vmem(5 + len(xts)),
            out_specs=vmem(1 + len(xts)),
            compiler_params=params,
            name=f"later{batch}",
        )(info, pa, left, tiles, state, other, *xts)
        other = swap(state)
    state = jnp.transpose(state.reshape(points // LANES, m_dev * tpd, LANES), (1, 0, 2))
    return state.reshape(m_dev, tpd, points)


def solution(mesh):
    return jax.shard_map(
        per_device,
        mesh=mesh,
        in_specs=(
            P("mem", ("tile", "obs"), None),
            P("obs", "tile"),
            P("obs", "tile"),
            P("obs", "tile"),
        ),
        out_specs=P("mem", ("tile", "obs"), None),
        check_vma=False,
    )
```

```python
import functools

import jax
import jax.numpy as jnp
from jax import lax
from jax.experimental import pallas as pl
from jax.experimental.pallas import tpu as pltpu
from jax.sharding import PartitionSpec as P

LANES = 128
WIDTH = 256
VALUE, VAR, TILE = 0, 1, 2
MIB = 1024 * 1024
F32, BF16 = jnp.float32, jnp.bfloat16


def halves(x):
    high = x.astype(BF16)
    return high, (x - high.astype(F32)).astype(BF16)


def nn_dot(a, b):
    return jnp.dot(a, b, preferred_element_type=F32)


def nt_dot(a, b):
    return lax.dot_general(a, b, (((1,), (1,)), ((), ())), preferred_element_type=F32)


def taper(place_a, place_b):
    delta = jnp.abs(place_a - place_b)
    z = jnp.minimum(delta, 2.0 - delta)
    return (((-0.25 * z + 0.5) * z + 0.625) * z - 5.0 / 3.0) * (z * z) + 1.0


def side(x):
    high, low = halves(x)
    return jnp.concatenate([high.astype(F32), low.astype(F32), high.astype(F32)], axis=1).astype(BF16)


def stacked(x):
    high, low = halves(x)
    return jnp.concatenate([high, high, low], axis=0)


def pick_kernel(n_src, m_dev, tpd, n_dest, info, idx, *refs):
    chunks, (out, split, cols, picked) = refs[: 2 * n_src], refs[2 * n_src :]
    core = info[1]
    members = 2 * m_dev
    points = chunks[0].shape[1]
    for src in range(n_src):
        for part in range(points // LANES):
            lanes = pl.ds(part * LANES, LANES)
            split[0] = chunks[src][:, lanes]
            split[1] = chunks[n_src + src][:, lanes]
            for tile in range(tpd):
                rows = pl.ds(tile, m_dev, stride=tpd)
                a, b = split[0, rows, :], split[1, rows, :]
                block = jnp.concatenate(
                    [
                        jnp.where(core == 0, a, b),
                        jnp.where(core == 0, b, a),
                        jnp.zeros((LANES - members, LANES), F32),
                    ],
                    axis=0,
                )
                start = (src * tpd + tile) * points + part * LANES
                cols[pl.ds(start, LANES), :] = block.T
    cols[pl.ds(n_src * tpd * points, 8), :] = jnp.zeros((8, LANES), F32)

    def body(step, carry):
        base = pl.multiple_of(step * 16, 16)
        for row in range(16):
            picked[pl.ds(base + row, 1), :] = cols[pl.ds(idx[base + row], 1), :]
        return carry

    lax.fori_loop(0, picked.shape[0] // 16, body, 0)
    n = picked.shape[0] // n_dest
    spare = lax.broadcasted_iota(jnp.int32, (8, LANES), 1) >= members
    for dest in range(n_dest):
        tail = picked[pl.ds(dest * n + n - 8, 8), :]
        one = jnp.where(spare, pltpu.roll(tail, members, 1), picked[pl.ds(dest * n, 8), :])
        rest = 2 * members - LANES
        two = jnp.where(spare, pltpu.roll(tail, rest, 1), picked[pl.ds(dest * n + 8, 8), :])
        out[pl.ds(dest * (n - 8), 8), :] = one
        out[pl.ds(dest * (n - 8) + 8, 8), :] = two
        out[pl.ds(dest * (n - 8) + 16, n - 24), :] = picked[pl.ds(dest * n + 16, n - 24), :]


def weights(block, members):
    x = block[:members]
    mean = jnp.sum(x, axis=0, keepdims=True) / members
    pa = x - mean
    value = block[members + VALUE : members + VALUE + 1]
    var = block[members + VAR : members + VAR + 1]
    places = block[members + TILE : members + TILE + 1]
    total_var = jnp.sum(pa * pa, axis=0, keepdims=True) / (members - 1) + var
    alpha = 1.0 / (1.0 + jnp.sqrt(var / total_var))
    weight_a = alpha / total_var
    weight_d = (value - mean) / total_var
    left = (weight_d - weight_a * pa) / (members - 1)
    return pa, left, places


def add_block(acc, rows_x, pa3, left2, places, own_places):
    members = left2.shape[0] // 2
    high, low = halves(taper(own_places, places) * nn_dot(rows_x, pa3))
    return acc[0] + nt_dot(high, left2), acc[1] + nt_dot(low, left2[:members])


def zero_acc(n, members):
    return jnp.zeros((n, 2 * members), F32), jnp.zeros((n, members), F32)


def summed(acc):
    members = acc[1].shape[1]
    return acc[0][:, :members] + acc[0][:, members:] + acc[1]


def next_kernel(members, own4, oth4, xt_ref, q_out, pa3_out, left_out, place_out):
    xt = xt_ref[...]
    rows_x = side(xt[:, :members])
    own_places = xt[:, members + TILE : members + TILE + 1]
    acc = zero_acc(WIDTH, members)
    n_block = 4
    for at in range(2 * n_block):
        block = (own4 if at < n_block else oth4)[at % n_block]
        pa, left, places = weights(block, members)
        pa3, left2 = stacked(pa), jnp.concatenate(halves(left), axis=0)
        acc = add_block(acc, rows_x, pa3, left2, places, own_places)
        cols = pl.ds(at * WIDTH, WIDTH)
        pa3_out[:, cols] = pa3
        left_out[:, cols] = left
        place_out[:, cols] = places
    pad = jnp.zeros((WIDTH, LANES - members), F32)
    new = xt + jnp.concatenate([summed(acc), pad], axis=1)
    q_out[...] = new.T[: q_out.shape[0]]


def state_part(members, tpd, info, pa3_ref, left_ref, place_ref, own, other, new, split, total):
    m_dev = members // 2
    n_obs = pa3_ref.shape[1]
    first, core = info[0], info[1]
    start = pl.multiple_of(core * m_dev, 8)
    gram = jnp.zeros((tpd * m_dev, 2 * members), F32)
    extra = jnp.zeros((tpd * m_dev, members), F32)
    for at in range(n_obs // WIDTH):
        cols = pl.ds(at * WIDTH, WIDTH)
        left = left_ref[pl.ds(start, m_dev), cols]
        places = place_ref[:, cols]
        scaled = jnp.concatenate(
            [
                left * taper((first + tile).astype(F32) * (2.0 / total), places)
                for tile in range(tpd)
            ],
            axis=0,
        )
        high, low = halves(scaled)
        pa3 = pa3_ref[:, cols]
        gram += nt_dot(high, pa3[members:])
        extra += nt_dot(low, pa3[:members])
    gram = side(gram[:, :members] + gram[:, members:] + extra)
    n_part = own.shape[1] // LANES
    for part in range(n_part):
        lanes = pl.ds(part * LANES, LANES)
        split[part] = own[:, lanes]
        split[n_part + part] = other[:, lanes]
    for tile in range(tpd):
        rows = pl.ds(tile, m_dev, stride=tpd)
        a = jnp.concatenate([split[part, rows, :] for part in range(n_part)], axis=1)
        b = jnp.concatenate([split[n_part + part, rows, :] for part in range(n_part)], axis=1)
        whole = jnp.concatenate([jnp.where(core == 0, a, b), jnp.where(core == 0, b, a)], axis=0)
        got = a + nn_dot(gram[tile * m_dev : (tile + 1) * m_dev], stacked(whole))
        for part in range(n_part):
            split[part, rows, :] = got[:, part * LANES : (part + 1) * LANES]
    for part in range(n_part):
        new[:, pl.ds(part * LANES, LANES)] = split[part]


def later_kernel(members, total, tpd, info, pa3_ref, left_ref, place_ref, own, other, *refs):
    refs, split = refs[:-1], refs[-1]
    n_later = (len(refs) - 1) // 2
    xts, outs, new = refs[:n_later], refs[n_later : 2 * n_later], refs[-1]
    n_obs = pa3_ref.shape[1]
    for xt_ref, out in zip(xts, outs):
        xt = xt_ref[...]
        rows_x = side(xt[:, :members])
        own_places = xt[:, members + TILE : members + TILE + 1]
        acc = zero_acc(WIDTH, members)
        for at in range(n_obs // WIDTH):
            cols = pl.ds(at * WIDTH, WIDTH)
            left2 = jnp.concatenate(halves(left_ref[:, cols]), axis=0)
            acc = add_block(acc, rows_x, pa3_ref[:, cols], left2, place_ref[:, cols], own_places)
        pad = jnp.zeros((WIDTH, LANES - members), F32)
        out[...] = xt + jnp.concatenate([summed(acc), pad], axis=1)
    state_part(members, tpd, info, pa3_ref, left_ref, place_ref, own, other, new, split, total)


def last_kernel(members, total, tpd, info, own4, oth4, own, other, new, pa_s, left_s, place_s, split):
    n_block = 4
    for at in range(2 * n_block):
        block = (own4 if at < n_block else oth4)[at % n_block]
        pa, left, places = weights(block, members)
        cols = pl.ds(at * WIDTH, WIDTH)
        pa_s[:, cols] = stacked(pa)
        left_s[:, cols] = left
        place_s[:, cols] = places
    state_part(members, tpd, info, pa_s, left_s, place_s, own, other, new, split, total)


def vmem(n):
    return [pl.BlockSpec(memory_space=pltpu.VMEM)] * n


def smem(n):
    return [pl.BlockSpec(memory_space=pltpu.SMEM)] * n


def out_f32(*shape):
    return jax.ShapeDtypeStruct(shape, F32)


def ring(n, shift):
    return [(i, (i + shift) % n) for i in range(n)]


def call(kernel, name, n_smem, n_vmem, outs, flops, scratch=()):
    return pl.pallas_call(
        kernel,
        out_shape=outs,
        in_specs=smem(n_smem) + vmem(n_vmem),
        out_specs=vmem(len(outs)) if isinstance(outs, list) else vmem(1)[0],
        scratch_shapes=list(scratch),
        compiler_params=pltpu.CompilerParams(vmem_limit_bytes=24 * MIB),
        cost_estimate=pl.CostEstimate(flops=flops, bytes_accessed=4 * MIB, transcendentals=0),
        name=name,
    )


def per_device(ensemble, obs_cell, obs_value, obs_var):
    m_dev, tpd, points = ensemble.shape
    n_tile = lax.axis_size("tile")
    n_obs = lax.axis_size("obs")
    members = 2 * m_dev
    per_dev = obs_cell.shape[1]
    half = per_dev // 2
    part = half // n_obs
    batch_obs = per_dev * n_tile
    height = members + 8
    total = tpd * n_tile * n_obs
    slab_cells = tpd * points
    tile_at, obs_at, core = (lax.axis_index(a) for a in ("tile", "obs", "mem"))
    first_tile = (tile_at * n_obs + obs_at) * tpd
    info = jnp.stack([first_tile, core]).astype(jnp.int32)
    swap = functools.partial(lax.ppermute, axis_name="mem", perm=[(0, 1), (1, 0)])

    def shifted(x):
        return [x] + [lax.ppermute(x, "obs", ring(n_obs, k)) for k in range(1, n_obs)]

    def own_half(x):
        return lax.dynamic_slice(x, (0, core * half), (1, half)).reshape(half, 1)

    state = ensemble.reshape(m_dev * tpd, points)
    chunks = shifted(state)
    others = [swap(chunk) for chunk in chunks]

    cells = obs_cell.astype(F32)
    sent = jnp.broadcast_to(jnp.concatenate([cells, cells], axis=1)[None], (n_tile, 1, 2 * per_dev))
    cells = lax.all_to_all(sent, "tile", 0, 0)
    cells = lax.dynamic_slice(cells, (0, 0, core * half), (n_tile, 1, half))
    cells = cells.reshape(n_tile * half).astype(jnp.int32)
    slab = cells // slab_cells
    source = (obs_at - slab % n_obs + n_obs) % n_obs
    idx = jnp.where(
        slab // n_obs == tile_at, source * slab_cells + cells % slab_cells, n_obs * slab_cells
    )

    picked = call(
        functools.partial(pick_kernel, n_obs, m_dev, tpd, n_tile),
        "pick",
        2,
        2 * n_obs,
        out_f32(n_tile * (half - 8), LANES),
        10**9,
        [
            pltpu.VMEM((2, m_dev * tpd, LANES), F32),
            pltpu.VMEM((n_obs * slab_cells + 8, LANES), F32),
            pltpu.VMEM((n_tile * half, LANES), F32),
        ],
    )(info, idx, *chunks, *others)
    rows = jnp.sum(lax.all_to_all(picked.reshape(n_tile, half - 8, LANES), "tile", 0, 0), axis=0)
    rest = 2 * members - LANES
    tail = [rows[:8, members:], rows[8:16, members : members + rest], rows[:8, members:]]
    rows = jnp.concatenate([rows, jnp.concatenate(tail, axis=1)], axis=0)
    lane = lax.broadcasted_iota(jnp.int32, (half, LANES), 1)
    rows = jnp.where(lane < members, rows, 0.0)
    place = (obs_cell // points).astype(F32) * (2.0 / total)
    for at, x in ((VALUE, obs_value), (VAR, obs_var), (TILE, place)):
        rows = jnp.where(lane == members + at, own_half(x), rows)
    sent = jnp.broadcast_to(rows.reshape(1, n_obs, part, LANES), (n_tile, n_obs, part, LANES))
    got = lax.all_to_all(sent.reshape(n_tile * n_obs, part, LANES), ("tile", "obs"), 0, 0)
    got = got.reshape(n_tile, n_obs, part, LANES)
    xts = [got[:, b].reshape(WIDTH, LANES) for b in range(n_obs)]
    own4 = jnp.stack(shifted(xts[0].T[:height]))
    oth4 = swap(own4)
    xts = xts[1:]

    other = others[0]
    split = pltpu.VMEM((2 * points // LANES, m_dev * tpd, LANES), F32)
    for batch in range(n_obs - 1):
        q, pa3, left, places = call(
            functools.partial(next_kernel, members),
            f"next{batch}",
            0,
            3,
            [
                out_f32(height, WIDTH),
                jax.ShapeDtypeStruct((3 * members, batch_obs), BF16),
                out_f32(members, batch_obs),
                out_f32(1, batch_obs),
            ],
            2 * 10**9,
        )(own4, oth4, xts[0])
        own4 = jnp.stack(shifted(q))
        xts = xts[1:]
        *xts, state = call(
            functools.partial(later_kernel, members, total, tpd),
            f"later{batch}",
            1,
            5 + len(xts),
            [out_f32(WIDTH, LANES)] * len(xts) + [out_f32(*state.shape)],
            8 * 10**9,
            [split],
        )(info, pa3, left, places, state, other, *xts)
        own4, state = lax.optimization_barrier((own4, state))
        oth4, other = swap(own4), swap(state)
    state = call(
        functools.partial(last_kernel, members, total, tpd),
        "last",
        1,
        4,
        out_f32(*state.shape),
        4 * 10**9,
        [
            pltpu.VMEM((3 * members, batch_obs), BF16),
            pltpu.VMEM((members, batch_obs), F32),
            pltpu.VMEM((1, batch_obs), F32),
            split,
        ],
    )(info, own4, oth4, state, other)
    return state.reshape(m_dev, tpd, points)


def solution(mesh):
    return jax.shard_map(
        per_device,
        mesh=mesh,
        in_specs=(
            P("mem", ("tile", "obs"), None),
            P("obs", "tile"),
            P("obs", "tile"),
            P("obs", "tile"),
        ),
        out_specs=P("mem", ("tile", "obs"), None),
        check_vma=False,
    )
```

```python
import functools

import jax
import jax.numpy as jnp
from jax import lax
from jax.experimental import pallas as pl
from jax.experimental.pallas import tpu as pltpu
from jax.sharding import PartitionSpec as P

LANES = 128
WIDTH = 256
ROOM, SENT = 56, 40
VALUE, VAR, TILE = 0, 1, 2
MIB = 1024 * 1024
F32, BF16 = jnp.float32, jnp.bfloat16


def halves(x):
    high = x.astype(BF16)
    return high, (x - high.astype(F32)).astype(BF16)


def nn_dot(a, b):
    return jnp.dot(a, b, preferred_element_type=F32)


def nt_dot(a, b):
    return lax.dot_general(a, b, (((1,), (1,)), ((), ())), preferred_element_type=F32)


def taper(place_a, place_b):
    delta = jnp.abs(place_a - place_b)
    z = jnp.minimum(delta, 2.0 - delta)
    return (((-0.25 * z + 0.5) * z + 0.625) * z - 5.0 / 3.0) * (z * z) + 1.0


def side(x):
    high, low = halves(x)
    return jnp.concatenate([high.astype(F32), low.astype(F32), high.astype(F32)], axis=1).astype(BF16)


def stacked(x):
    high, low = halves(x)
    return jnp.concatenate([high, high, low], axis=0)


def pick_kernel(n_src, m_dev, tpd, info, idx, *refs):
    chunks, (first, out, split, cols) = refs[: 2 * n_src], refs[2 * n_src :]
    core = info[1]
    members = 2 * m_dev
    points = chunks[0].shape[1]
    for src in range(n_src):
        for part in range(points // LANES):
            lanes = pl.ds(part * LANES, LANES)
            split[0] = chunks[src][:, lanes]
            split[1] = chunks[n_src + src][:, lanes]
            for tile in range(tpd):
                rows = pl.ds(tile, m_dev, stride=tpd)
                a, b = split[0, rows, :], split[1, rows, :]
                block = jnp.concatenate(
                    [
                        jnp.where(core == 0, a, b),
                        jnp.where(core == 0, b, a),
                        jnp.zeros((LANES - members, LANES), F32),
                    ],
                    axis=0,
                )
                start = (src * tpd + tile) * points + part * LANES
                cols[pl.ds(start, LANES), :] = block.T
    held = n_src * tpd * points
    cols[pl.ds(held, 8), :] = jnp.zeros((8, LANES), F32)
    unused = out.shape[0] - 8

    def body(step, rank):
        base = pl.multiple_of(step * 16, 16)
        sources = [idx[base + row] for row in range(16)]
        rows = [cols[pl.ds(at, 1), :] for at in sources]
        for at, row in zip(sources, rows):
            out[pl.ds(jnp.where(at < held, rank, unused), 1), :] = row
            rank = rank + (at < held).astype(jnp.int32)
        return rank

    lax.fori_loop(0, idx.shape[0] // 16, body, jnp.int32(0))
    pack_rows(out, first, members)


def pack_rows(rows, sent, members):
    sent[...] = rows[pl.ds(0, SENT), :]
    spare = lax.broadcasted_iota(jnp.int32, (8, LANES), 1) >= members
    for at in range((ROOM - SENT) // 8):
        tail = rows[pl.ds(SENT + 8 * at, 8), :]
        for half, shift in enumerate((members, 2 * members - LANES)):
            own = pl.ds(16 * at + 8 * half, 8)
            sent[own, :] = jnp.where(spare, pltpu.roll(tail, shift, 1), sent[own, :])


def unpack_rows(sent, rows, members):
    split = LANES - members
    lane = lax.broadcasted_iota(jnp.int32, (8, LANES), 1)
    for who in range(sent.shape[0]):
        rows[pl.ds(who * ROOM, SENT), :] = sent[who]
        for at in range((ROOM - SENT) // 8):
            one = pltpu.roll(sent[who, pl.ds(16 * at, 8), :], split, 1)
            two = pltpu.roll(sent[who, pl.ds(16 * at + 8, 8), :], 2 * split, 1)
            rows[pl.ds(who * ROOM + SENT + 8 * at, 8), :] = jnp.where(lane < split, one, two)


def repack_kernel(members, held, out):
    pack_rows(held, out, members)


def place_kernel(n_tile, room, owner, source, ranks, rounds, count):
    for at in range(n_tile):
        count[at] = 0

    def body(step, most):
        for part in range(8):
            row = step * 8 + part
            who = owner[row]
            rank = count[who]
            count[who] = rank + 1
            ranks[row] = rank
            source[row] = who * room + jnp.minimum(rank, room - 1)
            most = jnp.maximum(most, rank)
        return most

    rounds[0] = lax.fori_loop(0, owner.shape[0] // 8, body, jnp.int32(0)) // room + 1


def take_kernel(members, source, sent, rows, got):
    unpack_rows(sent, got, members)

    def body(step, carry):
        base = pl.multiple_of(step * 16, 16)
        for row in range(16):
            rows[pl.ds(base + row, 1), :] = got[pl.ds(source[base + row], 1), :]
        return carry

    lax.fori_loop(0, rows.shape[0] // 16, body, 0)


def retake_kernel(members, at, owner, ranks, sent, before, rows, got):
    unpack_rows(sent, got, members)
    rows[...] = before[...]
    room = ROOM

    def body(row, carry):
        rank = ranks[row] - at[0] * room

        @pl.when((rank >= 0) & (rank < room))
        def _():
            rows[pl.ds(row, 1), :] = got[pl.ds(owner[row] * room + rank, 1), :]

        return carry

    lax.fori_loop(0, rows.shape[0], body, 0)


def lists_kernel(cell, value, var, out, cells, reals, sems):
    copies = [
        pltpu.make_async_copy(cell, cells, sems.at[0]),
        pltpu.make_async_copy(value, reals.at[pl.ds(0, 1)], sems.at[1]),
        pltpu.make_async_copy(var, reals.at[pl.ds(1, 1)], sems.at[2]),
    ]
    for copy in copies:
        copy.start()
    for copy in copies:
        copy.wait()
    both = reals[...]
    first = jnp.concatenate([cells[...].astype(F32), both[:1]], axis=1)
    out[...] = jnp.concatenate([first, jnp.concatenate([both[1:], both[1:]], axis=1)], axis=0)


def columns_kernel(members, rows, meta, q):
    q[pl.ds(0, members), :] = rows[...].T[:members]
    q[pl.ds(members, 8), :] = meta[...]


def weights(block, members):
    x = block[:members]
    mean = jnp.sum(x, axis=0, keepdims=True) / members
    pa = x - mean
    value = block[members + VALUE : members + VALUE + 1]
    var = block[members + VAR : members + VAR + 1]
    places = block[members + TILE : members + TILE + 1]
    total_var = jnp.sum(pa * pa, axis=0, keepdims=True) / (members - 1) + var
    alpha = 1.0 / (1.0 + jnp.sqrt(var / total_var))
    weight_a = alpha / total_var
    weight_d = (value - mean) / total_var
    left = (weight_d - weight_a * pa) / (members - 1)
    return pa, left, places


def add_block(acc, rows_x, pa3, left2, places, own_places):
    members = left2.shape[0] // 2
    high, low = halves(taper(own_places, places) * nn_dot(rows_x, pa3))
    return acc[0] + nt_dot(high, left2), acc[1] + nt_dot(low, left2[:members])


def zero_acc(n, members):
    return jnp.zeros((n, 2 * members), F32), jnp.zeros((n, members), F32)


def summed(acc):
    members = acc[1].shape[1]
    return acc[0][:, :members] + acc[0][:, members:] + acc[1]


def next_kernel(members, own4, oth4, xt_ref, meta, q_out, pa3_out, left_out, place_out):
    xt = xt_ref[...]
    rows_x = side(xt[:, :members])
    own_places = meta[...].T[:, TILE : TILE + 1]
    acc = zero_acc(WIDTH, members)
    n_block = 4
    for at in range(2 * n_block):
        block = (own4 if at < n_block else oth4)[at % n_block]
        pa, left, places = weights(block, members)
        pa3, left2 = stacked(pa), jnp.concatenate(halves(left), axis=0)
        acc = add_block(acc, rows_x, pa3, left2, places, own_places)
        cols = pl.ds(at * WIDTH, WIDTH)
        pa3_out[:, cols] = pa3
        left_out[:, cols] = left
        place_out[:, cols] = places
    pad = jnp.zeros((WIDTH, LANES - members), F32)
    new = xt + jnp.concatenate([summed(acc), pad], axis=1)
    q_out[pl.ds(0, members), :] = new.T[:members]
    q_out[pl.ds(members, 8), :] = meta[...]


def state_part(members, tpd, info, pa3_ref, left_ref, place_ref, own, other, new, split, total):
    m_dev = members // 2
    n_obs = pa3_ref.shape[1]
    first, core = info[0], info[1]
    start = pl.multiple_of(core * m_dev, 8)
    gram = jnp.zeros((tpd * m_dev, 2 * members), F32)
    extra = jnp.zeros((tpd * m_dev, members), F32)
    for at in range(n_obs // WIDTH):
        cols = pl.ds(at * WIDTH, WIDTH)
        left = left_ref[pl.ds(start, m_dev), cols]
        places = place_ref[:, cols]
        scaled = jnp.concatenate(
            [
                left * taper((first + tile).astype(F32) * (2.0 / total), places)
                for tile in range(tpd)
            ],
            axis=0,
        )
        high, low = halves(scaled)
        pa3 = pa3_ref[:, cols]
        gram += nt_dot(high, pa3[members:])
        extra += nt_dot(low, pa3[:members])
    gram = side(gram[:, :members] + gram[:, members:] + extra)
    n_part = own.shape[1] // LANES
    for part in range(n_part):
        lanes = pl.ds(part * LANES, LANES)
        split[part] = own[:, lanes]
        split[n_part + part] = other[:, lanes]
    for tile in range(tpd):
        rows = pl.ds(tile, m_dev, stride=tpd)
        a = jnp.concatenate([split[part, rows, :] for part in range(n_part)], axis=1)
        b = jnp.concatenate([split[n_part + part, rows, :] for part in range(n_part)], axis=1)
        whole = jnp.concatenate([jnp.where(core == 0, a, b), jnp.where(core == 0, b, a)], axis=0)
        got = a + nn_dot(gram[tile * m_dev : (tile + 1) * m_dev], stacked(whole))
        for part in range(n_part):
            split[part, rows, :] = got[:, part * LANES : (part + 1) * LANES]
    for part in range(n_part):
        new[:, pl.ds(part * LANES, LANES)] = split[part]


def later_kernel(members, total, tpd, info, pa3_ref, left_ref, place_ref, own, other, *refs):
    refs, split = refs[:-1], refs[-1]
    n_later = (len(refs) - 1) // 3
    xts, metas, outs = refs[:n_later], refs[n_later : 2 * n_later], refs[2 * n_later : -1]
    new = refs[-1]
    n_obs = pa3_ref.shape[1]
    for xt_ref, meta, out in zip(xts, metas, outs):
        xt = xt_ref[...]
        rows_x = side(xt[:, :members])
        own_places = meta[...].T[:, TILE : TILE + 1]
        acc = zero_acc(WIDTH, members)
        for at in range(n_obs // WIDTH):
            cols = pl.ds(at * WIDTH, WIDTH)
            left2 = jnp.concatenate(halves(left_ref[:, cols]), axis=0)
            acc = add_block(acc, rows_x, pa3_ref[:, cols], left2, place_ref[:, cols], own_places)
        pad = jnp.zeros((WIDTH, LANES - members), F32)
        out[...] = xt + jnp.concatenate([summed(acc), pad], axis=1)
    state_part(members, tpd, info, pa3_ref, left_ref, place_ref, own, other, new, split, total)


def last_kernel(members, total, tpd, info, own4, oth4, own, other, new, pa_s, left_s, place_s, split):
    n_block = 4
    for at in range(2 * n_block):
        block = (own4 if at < n_block else oth4)[at % n_block]
        pa, left, places = weights(block, members)
        cols = pl.ds(at * WIDTH, WIDTH)
        pa_s[:, cols] = stacked(pa)
        left_s[:, cols] = left
        place_s[:, cols] = places
    state_part(members, tpd, info, pa_s, left_s, place_s, own, other, new, split, total)


def vmem(n):
    return [pl.BlockSpec(memory_space=pltpu.VMEM)] * n


def smem(n):
    return [pl.BlockSpec(memory_space=pltpu.SMEM)] * n


def out_f32(*shape):
    return jax.ShapeDtypeStruct(shape, F32)


def ring(n, shift):
    return [(i, (i + shift) % n) for i in range(n)]


def call(kernel, name, n_smem, n_vmem, outs, flops, scratch=(), out_specs=None, in_specs=None):
    return pl.pallas_call(
        kernel,
        out_shape=outs,
        in_specs=in_specs or smem(n_smem) + vmem(n_vmem),
        out_specs=out_specs or (vmem(len(outs)) if isinstance(outs, list) else vmem(1)[0]),
        scratch_shapes=list(scratch),
        compiler_params=pltpu.CompilerParams(vmem_limit_bytes=24 * MIB),
        cost_estimate=pl.CostEstimate(flops=flops, bytes_accessed=4 * MIB, transcendentals=0),
        name=name,
    )


def per_device(ensemble, obs_cell, obs_value, obs_var):
    m_dev, tpd, points = ensemble.shape
    n_tile = lax.axis_size("tile")
    n_obs = lax.axis_size("obs")
    members = 2 * m_dev
    per_dev = obs_cell.shape[1]
    quarter = per_dev // n_obs
    part = quarter // 2
    batch_obs = per_dev * n_tile
    height = members + 8
    total = tpd * n_tile * n_obs
    slab_cells = tpd * points
    tile_at, obs_at, core = (lax.axis_index(a) for a in ("tile", "obs", "mem"))
    first_tile = (tile_at * n_obs + obs_at) * tpd
    info = jnp.stack([first_tile, core]).astype(jnp.int32)
    swap = functools.partial(lax.ppermute, axis_name="mem", perm=[(0, 1), (1, 0)])

    def shifted(x):
        return [x] + [lax.ppermute(x, "obs", ring(n_obs, k)) for k in range(1, n_obs)]

    packed = call(
        lists_kernel,
        "lists",
        0,
        3,
        out_f32(2, 2 * per_dev),
        10**4,
        [
            pltpu.VMEM((1, per_dev), jnp.int32),
            pltpu.VMEM((2, per_dev), F32),
            pltpu.SemaphoreType.DMA((3,)),
        ],
        in_specs=[pl.BlockSpec(memory_space=pltpu.HBM)] * 3,
    )
    near = shifted(packed(obs_cell, obs_value, obs_var))
    state = ensemble.reshape(m_dev * tpd, points)
    chunks = shifted(state)
    others = [swap(chunk) for chunk in chunks]
    near = jnp.stack(near).reshape(n_obs, 4, per_dev)
    near = lax.dynamic_slice(near, (0, 0, obs_at * quarter), (n_obs, 4, quarter))
    sent = jnp.broadcast_to(near.reshape(1, 1, -1), (n_tile, 1, near.size))
    lists = lax.all_to_all(sent, "tile", 0, 0)
    lists = lists.reshape(n_tile, n_obs, 4, quarter)
    lists = lax.dynamic_slice(lists, (0, 0, 0, core * part), (n_tile, n_obs, 4, part))
    batches = []
    for batch in range(n_obs):
        at = (obs_at - batch + n_obs) % n_obs
        one = lax.dynamic_slice(lists, (0, at, 0, 0), (n_tile, 1, 4, part))
        batches.append(jnp.transpose(one.reshape(n_tile, 4, part), (1, 0, 2)).reshape(4, WIDTH))
    n_rows = n_obs * WIDTH
    cells = jnp.stack([one[0] for one in batches]).reshape(n_rows).astype(jnp.int32)
    metas = [
        jnp.concatenate(
            [
                one[1:3],
                (one[:1].astype(jnp.int32) // points).astype(F32) * (2.0 / total),
                jnp.zeros((5, WIDTH), F32),
            ],
            axis=0,
        )
        for one in batches
    ]

    slab = cells // slab_cells
    owner = slab // n_obs
    own = owner == tile_at
    near_at = (obs_at - slab % n_obs + n_obs) % n_obs
    idx = jnp.where(own, near_at * slab_cells + cells % slab_cells, n_obs * slab_cells)
    most_sends = -(-n_rows // ROOM)
    first, held = call(
        functools.partial(pick_kernel, n_obs, m_dev, tpd),
        "pick",
        2,
        2 * n_obs,
        [out_f32(SENT, LANES), out_f32(most_sends * ROOM + 8, LANES)],
        10**9,
        [
            pltpu.VMEM((2, m_dev * tpd, LANES), F32),
            pltpu.VMEM((n_obs * slab_cells + 8, LANES), F32),
        ],
    )(info, idx, *chunks, *others)
    first, owner, metas = lax.optimization_barrier((first, owner, metas))
    ints = [jax.ShapeDtypeStruct((n,), jnp.int32) for n in (n_rows, n_rows, 1)]
    source, ranks, rounds = call(
        functools.partial(place_kernel, n_tile, ROOM),
        "place",
        1,
        0,
        ints,
        10**9,
        [pltpu.SMEM((n_tile,), jnp.int32)],
        smem(3),
    )(owner)

    def send(rows):
        sent = jnp.broadcast_to(rows[None], (n_tile, SENT, LANES))
        return lax.all_to_all(sent, "tile", 0, 0)

    space = [pltpu.VMEM((n_tile * ROOM, LANES), F32)]
    take = functools.partial(take_kernel, members)
    rows = call(take, "take", 1, 1, out_f32(n_rows, LANES), 10**8, space)(source, send(first))

    def again(at, rows):
        more = lax.dynamic_slice(held, (at * ROOM, 0), (ROOM, LANES))
        repack = functools.partial(repack_kernel, members)
        got = send(call(repack, "repack", 0, 1, out_f32(SENT, LANES), 10**6)(more))
        retake = functools.partial(retake_kernel, members)
        return call(retake, "retake", 3, 2, out_f32(n_rows, LANES), 10**8, space)(
            at.reshape(1), owner, ranks, got, rows
        )

    rows = lax.fori_loop(jnp.int32(1), rounds[0], again, rows)
    xts = [rows[b * WIDTH : (b + 1) * WIDTH] for b in range(n_obs)]
    columns = functools.partial(columns_kernel, members)
    q = call(columns, "columns", 0, 2, out_f32(height, WIDTH), 10**7)(xts[0], metas[0])
    own4 = jnp.stack(shifted(q))
    oth4 = swap(own4)
    xts, metas = xts[1:], metas[1:]

    other = others[0]
    split = pltpu.VMEM((2 * points // LANES, m_dev * tpd, LANES), F32)
    for batch in range(n_obs - 1):
        q, pa3, left, places = call(
            functools.partial(next_kernel, members),
            f"next{batch}",
            0,
            4,
            [
                out_f32(height, WIDTH),
                jax.ShapeDtypeStruct((3 * members, batch_obs), BF16),
                out_f32(members, batch_obs),
                out_f32(1, batch_obs),
            ],
            2 * 10**9,
        )(own4, oth4, xts[0], metas[0])
        own4 = jnp.stack(shifted(q))
        xts, metas = xts[1:], metas[1:]
        *xts, state = call(
            functools.partial(later_kernel, members, total, tpd),
            f"later{batch}",
            1,
            5 + 2 * len(xts),
            [out_f32(WIDTH, LANES)] * len(xts) + [out_f32(*state.shape)],
            8 * 10**9,
            [split],
        )(info, pa3, left, places, state, other, *xts, *metas)
        own4, state = lax.optimization_barrier((own4, state))
        oth4, other = swap(own4), swap(state)
    state = call(
        functools.partial(last_kernel, members, total, tpd),
        "last",
        1,
        4,
        out_f32(*state.shape),
        4 * 10**9,
        [
            pltpu.VMEM((3 * members, batch_obs), BF16),
            pltpu.VMEM((members, batch_obs), F32),
            pltpu.VMEM((1, batch_obs), F32),
            split,
        ],
    )(info, own4, oth4, state, other)
    return state.reshape(m_dev, tpd, points)


def solution(mesh):
    return jax.shard_map(
        per_device,
        mesh=mesh,
        in_specs=(
            P("mem", ("tile", "obs"), None),
            P("obs", "tile"),
            P("obs", "tile"),
            P("obs", "tile"),
        ),
        out_specs=P("mem", ("tile", "obs"), None),
        check_vma=False,
    )
```

```python
import functools

import jax
import jax.numpy as jnp
from jax import lax
from jax.experimental import pallas as pl
from jax.experimental.pallas import tpu as pltpu
from jax.sharding import PartitionSpec as P

LANES = 128
WIDTH = 256
ROOM, SENT = 56, 40
VALUE, VAR, TILE = 0, 1, 2
MIB = 1024 * 1024
F32, BF16 = jnp.float32, jnp.bfloat16


def halves(x):
    high = x.astype(BF16)
    return high, (x - high.astype(F32)).astype(BF16)


def nn_dot(a, b):
    return jnp.dot(a, b, preferred_element_type=F32)


def nt_dot(a, b):
    return lax.dot_general(a, b, (((1,), (1,)), ((), ())), preferred_element_type=F32)


def taper(place_a, place_b):
    delta = jnp.abs(place_a - place_b)
    z = jnp.minimum(delta, 2.0 - delta)
    return (((-0.25 * z + 0.5) * z + 0.625) * z - 5.0 / 3.0) * (z * z) + 1.0


def side(x):
    high, low = halves(x)
    return jnp.concatenate([high.astype(F32), low.astype(F32), high.astype(F32)], axis=1).astype(BF16)


def stacked(x):
    high, low = halves(x)
    return jnp.concatenate([high, high, low], axis=0)


def split_kernel(state, out):
    rows, points = state.shape
    for part in range(points // LANES):
        out[pl.ds(part * rows, rows), :] = state[:, pl.ds(part * LANES, LANES)]


def pick_kernel(n_src, m_dev, tpd, info, masks, idx, *refs):
    chunks, (sent, out, cols) = refs[: 2 * n_src], refs[2 * n_src :]
    core = info[1]
    members = 2 * m_dev
    n_part = chunks[0].shape[0] // (m_dev * tpd)
    points = n_part * LANES
    for src in range(n_src):
        for part in range(n_part):
            for tile in range(tpd):
                rows = pl.ds(part * m_dev * tpd + tile, m_dev, stride=tpd)
                a, b = chunks[src][rows, :], chunks[n_src + src][rows, :]
                block = jnp.concatenate(
                    [
                        jnp.where(core == 0, a, b),
                        jnp.where(core == 0, b, a),
                        jnp.zeros((LANES - members, LANES), F32),
                    ],
                    axis=0,
                )
                start = (src * tpd + tile) * points + part * LANES
                cols[pl.ds(start, LANES), :] = block.T

    def one_tile(tile, rank):
        def one_row(carry):
            mask, rank = carry
            at = lax.clz(mask)
            out[pl.ds(rank, 1), :] = cols[pl.ds(idx[tile * 32 + at], 1), :]
            return mask ^ lax.shift_left(jnp.int32(1), 31 - at), rank + 1

        return lax.while_loop(lambda carry: carry[0] != 0, one_row, (masks[tile], rank))[1]

    lax.fori_loop(0, masks.shape[0], one_tile, jnp.int32(0))
    pack_rows(out, sent, members)


def pack_rows(rows, sent, members):
    packed = [rows[pl.ds(8 * at, 8), :] for at in range(SENT // 8)]
    spare = lax.broadcasted_iota(jnp.int32, (8, LANES), 1) >= members
    for at in range((ROOM - SENT) // 8):
        tail = rows[pl.ds(SENT + 8 * at, 8), :]
        for half, shift in enumerate((members, 2 * members - LANES)):
            here = 2 * at + half
            packed[here] = jnp.where(spare, pltpu.roll(tail, shift, 1), packed[here])
    for who in range(sent.shape[0]):
        for at, block in enumerate(packed):
            sent[who, pl.ds(8 * at, 8), :] = block


def unpack_rows(sent, rows, members):
    split = LANES - members
    lane = lax.broadcasted_iota(jnp.int32, (8, LANES), 1)
    for who in range(sent.shape[0]):
        rows[pl.ds(who * ROOM, SENT), :] = sent[who]
        for at in range((ROOM - SENT) // 8):
            one = pltpu.roll(sent[who, pl.ds(16 * at, 8), :], split, 1)
            two = pltpu.roll(sent[who, pl.ds(16 * at + 8, 8), :], 2 * split, 1)
            rows[pl.ds(who * ROOM + SENT + 8 * at, 8), :] = jnp.where(lane < split, one, two)


def repack_kernel(members, held, out):
    pack_rows(held, out, members)


def place_kernel(n_tile, owner, source, ranks, rounds, count):
    for at in range(n_tile):
        count[at] = 0

    def body(step, most):
        for part in range(8):
            row = step * 8 + part
            who = owner[row]
            rank = count[who]
            count[who] = rank + 1
            ranks[row] = rank
            source[row] = jnp.where(rank < ROOM, who * ROOM + rank, n_tile * ROOM + row)
            most = jnp.maximum(most, rank)
        return most

    rounds[0] = lax.fori_loop(0, owner.shape[0] // 8, body, jnp.int32(0)) // ROOM + 1


def rest_kernel(members, at, owner, ranks, sent, before, late, got):
    unpack_rows(sent, got, members)
    late[...] = before[...]

    def body(row, carry):
        rank = ranks[row] - at[0] * ROOM

        @pl.when((rank >= 0) & (rank < ROOM))
        def _():
            late[pl.ds(row, 1), :] = got[pl.ds(owner[row] * ROOM + rank, 1), :]

        return carry

    lax.fori_loop(0, late.shape[0], body, 0)


def take_rows(members, n_obs, part, batches, info, source, sent, late, outs, got):
    unpack_rows(sent, got, members)
    n_tile = sent.shape[0]
    got[pl.ds(n_tile * ROOM, late.shape[0]), :] = late[...]
    near = [lax.rem(info[2] - batch + n_obs, n_obs) for batch in batches]

    def body(step, carry):
        for half in range(2):
            who = step * 2 + half
            base = pl.multiple_of(step * 2 * part, 2 * part)
            for place, out in zip(near, outs):
                first = (who * n_obs + place) * part
                for row in range(part):
                    at = source[first + row]
                    out[pl.ds(base + half * part + row, 1), :] = got[pl.ds(at, 1), :]
        return carry

    lax.fori_loop(0, n_tile // 2, body, 0)


def first_kernel(members, n_obs, part, info, source, sent, late, meta, q, got, rows):
    take_rows(members, n_obs, part, [0], info, source, sent, late, [rows], got)
    q[pl.ds(0, members), :] = rows[...].T[:members]
    q[pl.ds(members, 8), :] = meta[...]


def others_kernel(members, n_obs, part, info, source, sent, late, *refs):
    take_rows(
        members, n_obs, part, range(1, n_obs), info, source, sent, late, refs[:-1], refs[-1]
    )


def weights(block, members):
    x = block[:members]
    mean = jnp.sum(x, axis=0, keepdims=True) / members
    pa = x - mean
    value = block[members + VALUE : members + VALUE + 1]
    var = block[members + VAR : members + VAR + 1]
    places = block[members + TILE : members + TILE + 1]
    total_var = jnp.sum(pa * pa, axis=0, keepdims=True) / (members - 1) + var
    alpha = 1.0 / (1.0 + jnp.sqrt(var / total_var))
    weight_a = alpha / total_var
    weight_d = (value - mean) / total_var
    left = (weight_d - weight_a * pa) / (members - 1)
    return pa, left, places


def add_block(acc, rows_x, pa3, left2, places, own_places):
    members = left2.shape[0] // 2
    high, low = halves(taper(own_places, places) * nn_dot(rows_x, pa3))
    return acc[0] + nt_dot(high, left2), acc[1] + nt_dot(low, left2[:members])


def zero_acc(n, members):
    return jnp.zeros((n, 2 * members), F32), jnp.zeros((n, members), F32)


def summed(acc):
    members = acc[1].shape[1]
    return acc[0][:, :members] + acc[0][:, members:] + acc[1]


def next_kernel(members, own4, oth4, xt_ref, meta, q_out, pa3_out, left_out, place_out):
    xt = xt_ref[...]
    rows_x = side(xt[:, :members])
    own_places = meta[...].T[:, TILE : TILE + 1]
    acc = zero_acc(WIDTH, members)
    n_block = 4
    for at in range(2 * n_block):
        block = (own4 if at < n_block else oth4)[at % n_block]
        pa, left, places = weights(block, members)
        pa3, left2 = stacked(pa), jnp.concatenate(halves(left), axis=0)
        acc = add_block(acc, rows_x, pa3, left2, places, own_places)
        cols = pl.ds(at * WIDTH, WIDTH)
        pa3_out[:, cols] = pa3
        left_out[:, cols] = left
        place_out[:, cols] = places
    pad = jnp.zeros((WIDTH, LANES - members), F32)
    new = xt + jnp.concatenate([summed(acc), pad], axis=1)
    q_out[pl.ds(0, members), :] = new.T[:members]
    q_out[pl.ds(members, 8), :] = meta[...]


def state_part(members, tpd, info, pa3_ref, left_ref, place_ref, own, other, new, total):
    m_dev = members // 2
    n_obs = pa3_ref.shape[1]
    first, core = info[0], info[1]
    start = pl.multiple_of(core * m_dev, 8)
    gram = jnp.zeros((tpd * m_dev, 2 * members), F32)
    extra = jnp.zeros((tpd * m_dev, members), F32)
    for at in range(n_obs // WIDTH):
        cols = pl.ds(at * WIDTH, WIDTH)
        left = left_ref[pl.ds(start, m_dev), cols]
        places = place_ref[:, cols]
        scaled = jnp.concatenate(
            [
                left * taper((first + tile).astype(F32) * (2.0 / total), places)
                for tile in range(tpd)
            ],
            axis=0,
        )
        high, low = halves(scaled)
        pa3 = pa3_ref[:, cols]
        gram += nt_dot(high, pa3[members:])
        extra += nt_dot(low, pa3[:members])
    gram = side(gram[:, :members] + gram[:, members:] + extra)
    n_part = own.shape[0] // (m_dev * tpd)
    for tile in range(tpd):
        rows = [pl.ds(part * m_dev * tpd + tile, m_dev, stride=tpd) for part in range(n_part)]
        a = jnp.concatenate([own[row, :] for row in rows], axis=1)
        b = jnp.concatenate([other[row, :] for row in rows], axis=1)
        whole = jnp.concatenate([jnp.where(core == 0, a, b), jnp.where(core == 0, b, a)], axis=0)
        got = a + nn_dot(gram[tile * m_dev : (tile + 1) * m_dev], stacked(whole))
        for part, row in enumerate(rows):
            new[row, :] = got[:, part * LANES : (part + 1) * LANES]


def later_kernel(members, total, tpd, info, pa3_ref, left_ref, place_ref, own, other, *refs):
    n_later = (len(refs) - 1) // 3
    xts, metas, outs = refs[:n_later], refs[n_later : 2 * n_later], refs[2 * n_later : -1]
    new = refs[-1]
    n_obs = pa3_ref.shape[1]
    for xt_ref, meta, out in zip(xts, metas, outs):
        xt = xt_ref[...]
        rows_x = side(xt[:, :members])
        own_places = meta[...].T[:, TILE : TILE + 1]
        acc = zero_acc(WIDTH, members)
        for at in range(n_obs // WIDTH):
            cols = pl.ds(at * WIDTH, WIDTH)
            left2 = jnp.concatenate(halves(left_ref[:, cols]), axis=0)
            acc = add_block(acc, rows_x, pa3_ref[:, cols], left2, place_ref[:, cols], own_places)
        pad = jnp.zeros((WIDTH, LANES - members), F32)
        out[...] = xt + jnp.concatenate([summed(acc), pad], axis=1)
    state_part(members, tpd, info, pa3_ref, left_ref, place_ref, own, other, new, total)


def last_kernel(members, total, tpd, info, own4, oth4, own, other, out, pa_s, left_s, place_s, new):
    n_block = 4
    for at in range(2 * n_block):
        block = (own4 if at < n_block else oth4)[at % n_block]
        pa, left, places = weights(block, members)
        cols = pl.ds(at * WIDTH, WIDTH)
        pa_s[:, cols] = stacked(pa)
        left_s[:, cols] = left
        place_s[:, cols] = places
    state_part(members, tpd, info, pa_s, left_s, place_s, own, other, new, total)
    rows = out.shape[0]
    for part in range(new.shape[0] // rows):
        out[:, pl.ds(part * LANES, LANES)] = new[pl.ds(part * rows, rows), :]


def vmem(n):
    return [pl.BlockSpec(memory_space=pltpu.VMEM)] * n


def smem(n):
    return [pl.BlockSpec(memory_space=pltpu.SMEM)] * n


def out_f32(*shape):
    return jax.ShapeDtypeStruct(shape, F32)


def ring(n, shift):
    return [(i, (i + shift) % n) for i in range(n)]


def call(kernel, name, n_smem, n_vmem, outs, flops, scratch=(), out_specs=None):
    return pl.pallas_call(
        kernel,
        out_shape=outs,
        in_specs=smem(n_smem) + vmem(n_vmem),
        out_specs=out_specs or (vmem(len(outs)) if isinstance(outs, list) else vmem(1)[0]),
        scratch_shapes=list(scratch),
        compiler_params=pltpu.CompilerParams(vmem_limit_bytes=24 * MIB),
        cost_estimate=pl.CostEstimate(flops=flops, bytes_accessed=4 * MIB, transcendentals=0),
        name=name,
    )


def per_device(ensemble, obs_cell, obs_value, obs_var):
    m_dev, tpd, points = ensemble.shape
    n_tile = lax.axis_size("tile")
    n_obs = lax.axis_size("obs")
    members = 2 * m_dev
    per_dev = obs_cell.shape[1]
    half = per_dev // 2
    part = half // n_obs
    batch_obs = per_dev * n_tile
    height = members + 8
    total = tpd * n_tile * n_obs
    slab_cells = tpd * points
    tile_at, obs_at, core = (lax.axis_index(a) for a in ("tile", "obs", "mem"))
    first_tile = (tile_at * n_obs + obs_at) * tpd
    info = jnp.stack([first_tile, core, obs_at]).astype(jnp.int32)
    swap = functools.partial(lax.ppermute, axis_name="mem", perm=[(0, 1), (1, 0)])

    def shifted(x):
        return [x] + [lax.ppermute(x, "obs", ring(n_obs, k)) for k in range(1, n_obs)]

    def own_half(x):
        return lax.dynamic_slice(x, (0, core * half), (1, half))

    kind = lax.broadcasted_iota(jnp.int32, (4, half), 0)
    packed = jnp.where(kind == 1, own_half(obs_value), own_half(obs_var))
    packed = jnp.where(kind == 0, own_half(obs_cell).astype(F32), packed)
    near = shifted(packed)
    flat = (m_dev * tpd * points // LANES, LANES)
    split = call(split_kernel, "split", 0, 1, out_f32(*flat), 10**6)
    state = split(ensemble.reshape(m_dev * tpd, points))
    chunks = shifted(state)
    others = [swap(chunk) for chunk in chunks]
    near = lax.dynamic_slice(jnp.stack(near, axis=1), (0, 0, obs_at * part), (4, n_obs, part))
    sent = jnp.broadcast_to(near.reshape(1, 1, -1), (n_tile, 1, near.size))
    lists = lax.all_to_all(sent, "tile", 0, 0)

    n_rows = n_tile * half
    cells = lists[:, 0, :half].reshape(n_rows).astype(jnp.int32)
    slab = cells // slab_cells
    owner = slab // n_obs
    near_at = (obs_at - slab % n_obs + n_obs) % n_obs
    idx = near_at * slab_cells + cells % slab_cells
    own = (lists[:, 0, :half].astype(jnp.int32) // (slab_cells * n_obs) == tile_at).astype(jnp.int32)
    masks = jnp.sum(lax.shift_left(own, 31 - lax.broadcasted_iota(jnp.int32, own.shape, 1)), axis=1)
    most_sends = -(-n_rows // ROOM)
    first, held = call(
        functools.partial(pick_kernel, n_obs, m_dev, tpd),
        "pick",
        3,
        2 * n_obs,
        [out_f32(n_tile, SENT, LANES), out_f32(most_sends * ROOM, LANES)],
        10**9,
        [
            pltpu.VMEM((n_obs * slab_cells, LANES), F32),
        ],
    )(info, masks, idx, *chunks, *others)
    first, owner, lists = lax.optimization_barrier((first, owner, lists))
    ints = [jax.ShapeDtypeStruct((n,), jnp.int32) for n in (n_rows, n_rows, 1)]
    source, ranks, rounds = call(
        functools.partial(place_kernel, n_tile),
        "place",
        1,
        0,
        ints,
        10**9,
        [pltpu.SMEM((n_tile,), jnp.int32)],
        smem(3),
    )(owner)
    lists = jnp.transpose(lists.reshape(n_tile, 4, n_obs, part), (2, 1, 0, 3))
    lists = lists.reshape(n_obs, 4, WIDTH)
    metas = []
    for batch in range(n_obs):
        at = (obs_at - batch + n_obs) % n_obs
        one = lax.dynamic_slice(lists, (at, 0, 0), (1, 4, WIDTH))[0]
        place = (one[:1].astype(jnp.int32) // points).astype(F32) * (2.0 / total)
        metas.append(jnp.concatenate([one[1:3], place, jnp.zeros((5, WIDTH), F32)], axis=0))

    space = [pltpu.VMEM((n_tile * ROOM + n_rows, LANES), F32)]
    got = lax.all_to_all(first, "tile", 0, 0)

    def again(at, late):
        more = lax.dynamic_slice(held, (at * ROOM, 0), (ROOM, LANES))
        repack = functools.partial(repack_kernel, members)
        more = call(repack, "repack", 0, 1, out_f32(n_tile, SENT, LANES), 10**6)(more)
        got = lax.all_to_all(more, "tile", 0, 0)
        rest = functools.partial(rest_kernel, members)
        return call(rest, "rest", 3, 2, out_f32(n_rows, LANES), 10**8, space)(
            at.reshape(1), owner, ranks, got, late
        )

    got, late = lax.optimization_barrier((got, jnp.zeros((n_rows, LANES), F32)))
    late = lax.fori_loop(jnp.int32(1), rounds[0], again, late)
    q = call(
        functools.partial(first_kernel, members, n_obs, part),
        "first",
        2,
        3,
        out_f32(height, WIDTH),
        10**8,
        space + [pltpu.VMEM((WIDTH, LANES), F32)],
    )(info, source, got, late, metas[0])
    xts = call(
        functools.partial(others_kernel, members, n_obs, part),
        "others",
        2,
        2,
        [out_f32(WIDTH, LANES)] * (n_obs - 1),
        8 * 10**9,
        space,
    )(info, source, got, late)
    metas = metas[1:]
    own4 = jnp.stack(shifted(q))
    own4, xts = lax.optimization_barrier((own4, xts))
    oth4 = swap(own4)


    other = others[0]
    for batch in range(n_obs - 1):
        q, pa3, left, places = call(
            functools.partial(next_kernel, members),
            f"next{batch}",
            0,
            4,
            [
                out_f32(height, WIDTH),
                jax.ShapeDtypeStruct((3 * members, batch_obs), BF16),
                out_f32(members, batch_obs),
                out_f32(1, batch_obs),
            ],
            2 * 10**9,
        )(own4, oth4, xts[0], metas[0])
        own4 = jnp.stack(shifted(q))
        xts, metas = xts[1:], metas[1:]
        *xts, state = call(
            functools.partial(later_kernel, members, total, tpd),
            f"later{batch}",
            1,
            5 + 2 * len(xts),
            [out_f32(WIDTH, LANES)] * len(xts) + [out_f32(*state.shape)],
            8 * 10**9,
        )(info, pa3, left, places, state, other, *xts, *metas)
        own4, state = lax.optimization_barrier((own4, state))
        oth4, other = swap(own4), swap(state)
    state = call(
        functools.partial(last_kernel, members, total, tpd),
        "last",
        1,
        4,
        out_f32(m_dev * tpd, points),
        4 * 10**9,
        [
            pltpu.VMEM((3 * members, batch_obs), BF16),
            pltpu.VMEM((members, batch_obs), F32),
            pltpu.VMEM((1, batch_obs), F32),
            pltpu.VMEM(state.shape, F32),
        ],
    )(info, own4, oth4, state, other)
    return state.reshape(m_dev, tpd, points)


def solution(mesh):
    return jax.shard_map(
        per_device,
        mesh=mesh,
        in_specs=(
            P("mem", ("tile", "obs"), None),
            P("obs", "tile"),
            P("obs", "tile"),
            P("obs", "tile"),
        ),
        out_specs=P("mem", ("tile", "obs"), None),
        check_vma=False,
    )
```

```python
import functools

import jax
import jax.numpy as jnp
from jax import lax
from jax.experimental import pallas as pl
from jax.experimental.pallas import tpu as pltpu
from jax.sharding import PartitionSpec as P

LANES = 128
WIDTH = 256
ROOM, SENT = 56, 40
VALUE, VAR, TILE = 0, 1, 2
MIB = 1024 * 1024
F32, BF16 = jnp.float32, jnp.bfloat16


def halves(x):
    high = x.astype(BF16)
    return high, (x - high.astype(F32)).astype(BF16)


def nn_dot(a, b):
    return jnp.dot(a, b, preferred_element_type=F32)


def nt_dot(a, b):
    return lax.dot_general(a, b, (((1,), (1,)), ((), ())), preferred_element_type=F32)


def taper(place_a, place_b):
    delta = jnp.abs(place_a - place_b)
    z = jnp.minimum(delta, 2.0 - delta)
    return (((-0.25 * z + 0.5) * z + 0.625) * z - 5.0 / 3.0) * (z * z) + 1.0


def side(x):
    high, low = halves(x)
    return jnp.concatenate([high.astype(F32), low.astype(F32), high.astype(F32)], axis=1).astype(BF16)


def stacked(x):
    high, low = halves(x)
    return jnp.concatenate([high, high, low], axis=0)


def split_kernel(state, out):
    rows, points = state.shape
    for part in range(points // LANES):
        out[pl.ds(part * rows, rows), :] = state[:, pl.ds(part * LANES, LANES)]


def mix_kernel(part, info, *refs):
    lists, out = refs[:-1], refs[-1]
    fields, width = lists[0].shape
    lane = lax.broadcasted_iota(jnp.int32, (8, LANES), 1)
    mixed = jnp.zeros((8, LANES), F32)
    for at, ref in enumerate(lists):
        wide = jnp.concatenate([ref[...], jnp.zeros((fields, LANES - width), F32)], axis=1)
        wide = jnp.concatenate([wide, jnp.zeros((8 - fields, LANES), F32)], axis=0)
        moved = pltpu.roll(wide, lax.rem(LANES + (at - info[2]) * part, LANES), 1)
        mixed = jnp.where((lane >= at * part) & (lane < (at + 1) * part), moved, mixed)
    row = mixed[:1]
    for field in range(1, fields):
        row = row + pltpu.roll(mixed, field * width, 1)[field : field + 1]
    for who in range(out.shape[0]):
        out[who] = row


def find_kernel(n_src, slab_cells, half, info, lists, found):
    n_tile = lists.shape[0]
    cells = jnp.concatenate([lists[who] for who in range(n_tile)], axis=0).astype(jnp.int32)
    slab = lax.shift_right_logical(cells, slab_cells.bit_length() - 1)
    owner = lax.shift_right_logical(slab, n_src.bit_length() - 1)
    place = (info[2] - (slab & (n_src - 1)) + n_src) & (n_src - 1)
    lane = lax.broadcasted_iota(jnp.int32, cells.shape, 1)
    bits = jnp.where((owner == info[3]) & (lane < half), lax.shift_left(1, 15 - (lane & 15)), 0)
    bits = bits.astype(F32)
    upper = jnp.sum(jnp.where(lane < 16, bits, 0.0), axis=1, keepdims=True).astype(jnp.int32)
    lower = jnp.sum(jnp.where(lane >= 16, bits, 0.0), axis=1, keepdims=True).astype(jnp.int32)
    mask = lax.shift_left(upper, 16) | lower
    found[...] = jnp.where(lane < half, place * slab_cells + (cells & (slab_cells - 1)), mask)


def pick_kernel(n_src, m_dev, tpd, half, info, rows_at, *refs):
    chunks, (sent, out, cols) = refs[: 2 * n_src], refs[2 * n_src :]
    core = info[1]
    members = 2 * m_dev
    n_part = chunks[0].shape[0] // (m_dev * tpd)
    points = n_part * LANES
    for src in range(n_src):
        for part in range(n_part):
            for tile in range(tpd):
                rows = pl.ds(part * m_dev * tpd + tile, m_dev, stride=tpd)
                a, b = chunks[src][rows, :], chunks[n_src + src][rows, :]
                block = jnp.concatenate(
                    [
                        jnp.where(core == 0, a, b),
                        jnp.where(core == 0, b, a),
                        jnp.zeros((LANES - members, LANES), F32),
                    ],
                    axis=0,
                )
                start = (src * tpd + tile) * points + part * LANES
                cols[pl.ds(start, LANES), :] = block.T

    def one_tile(tile, rank):
        def one_row(carry):
            mask, rank = carry
            at = lax.clz(mask)
            out[pl.ds(rank, 1), :] = cols[pl.ds(rows_at[tile, at], 1), :]
            return mask ^ lax.shift_left(jnp.int32(1), 31 - at), rank + 1

        start = (rows_at[tile, half], rank)
        return lax.while_loop(lambda carry: carry[0] != 0, one_row, start)[1]

    lax.fori_loop(0, rows_at.shape[0], one_tile, jnp.int32(0))
    pack_rows(out, sent, members)


def pack_rows(rows, sent, members):
    packed = [rows[pl.ds(8 * at, 8), :] for at in range(SENT // 8)]
    spare = lax.broadcasted_iota(jnp.int32, (8, LANES), 1) >= members
    for at in range((ROOM - SENT) // 8):
        tail = rows[pl.ds(SENT + 8 * at, 8), :]
        for half, shift in enumerate((members, 2 * members - LANES)):
            here = 2 * at + half
            packed[here] = jnp.where(spare, pltpu.roll(tail, shift, 1), packed[here])
    for who in range(sent.shape[0]):
        for at, block in enumerate(packed):
            sent[who, pl.ds(8 * at, 8), :] = block


def unpack_rows(sent, rows, members):
    split = LANES - members
    lane = lax.broadcasted_iota(jnp.int32, (8, LANES), 1)
    for who in range(sent.shape[0]):
        rows[pl.ds(who * ROOM, SENT), :] = sent[who]
        for at in range((ROOM - SENT) // 8):
            one = pltpu.roll(sent[who, pl.ds(16 * at, 8), :], split, 1)
            two = pltpu.roll(sent[who, pl.ds(16 * at + 8, 8), :], 2 * split, 1)
            rows[pl.ds(who * ROOM + SENT + 8 * at, 8), :] = jnp.where(lane < split, one, two)


def repack_kernel(members, held, out):
    pack_rows(held, out, members)


def place_kernel(n_tile, owner, source, ranks, rounds, count):
    for at in range(n_tile):
        count[at] = 0

    def body(step, most):
        for part in range(8):
            row = step * 8 + part
            who = owner[row]
            rank = count[who]
            count[who] = rank + 1
            ranks[row] = rank
            source[row] = jnp.where(rank < ROOM, who * ROOM + rank, n_tile * ROOM + row)
            most = jnp.maximum(most, rank)
        return most

    rounds[0] = lax.fori_loop(0, owner.shape[0] // 8, body, jnp.int32(0)) // ROOM + 1


def rest_kernel(members, at, owner, ranks, sent, before, late, got):
    unpack_rows(sent, got, members)
    late[...] = before[...]

    def body(row, carry):
        rank = ranks[row] - at[0] * ROOM

        @pl.when((rank >= 0) & (rank < ROOM))
        def _():
            late[pl.ds(row, 1), :] = got[pl.ds(owner[row] * ROOM + rank, 1), :]

        return carry

    lax.fori_loop(0, late.shape[0], body, 0)


def take_rows(members, n_obs, part, batches, info, source, sent, late, outs, got):
    unpack_rows(sent, got, members)
    n_tile = sent.shape[0]
    got[pl.ds(n_tile * ROOM, late.shape[0]), :] = late[...]
    near = [lax.rem(info[2] - batch + n_obs, n_obs) for batch in batches]

    def body(step, carry):
        for half in range(2):
            who = step * 2 + half
            base = pl.multiple_of(step * 2 * part, 2 * part)
            for place, out in zip(near, outs):
                first = (who * n_obs + place) * part
                for row in range(part):
                    at = source[first + row]
                    out[pl.ds(base + half * part + row, 1), :] = got[pl.ds(at, 1), :]
        return carry

    lax.fori_loop(0, n_tile // 2, body, 0)


def first_kernel(members, n_obs, part, info, source, sent, late, meta, q, got, rows):
    take_rows(members, n_obs, part, [0], info, source, sent, late, [rows], got)
    q[pl.ds(0, members), :] = rows[...].T[:members]
    q[pl.ds(members, 8), :] = meta[...]


def others_kernel(members, n_obs, part, info, source, sent, late, *refs):
    take_rows(
        members, n_obs, part, range(1, n_obs), info, source, sent, late, refs[:-1], refs[-1]
    )


def weights(block, members):
    x = block[:members]
    mean = jnp.sum(x, axis=0, keepdims=True) / members
    pa = x - mean
    value = block[members + VALUE : members + VALUE + 1]
    var = block[members + VAR : members + VAR + 1]
    places = block[members + TILE : members + TILE + 1]
    total_var = jnp.sum(pa * pa, axis=0, keepdims=True) / (members - 1) + var
    alpha = 1.0 / (1.0 + jnp.sqrt(var / total_var))
    weight_a = alpha / total_var
    weight_d = (value - mean) / total_var
    left = (weight_d - weight_a * pa) / (members - 1)
    return pa, left, places


def add_block(acc, rows_x, pa3, left2, places, own_places):
    members = left2.shape[0] // 2
    high, low = halves(taper(own_places, places) * nn_dot(rows_x, pa3))
    return acc[0] + nt_dot(high, left2), acc[1] + nt_dot(low, left2[:members])


def zero_acc(n, members):
    return jnp.zeros((n, 2 * members), F32), jnp.zeros((n, members), F32)


def summed(acc):
    members = acc[1].shape[1]
    return acc[0][:, :members] + acc[0][:, members:] + acc[1]


def weigh(blocks, at, members, pa3_out, left_out, place_out):
    pa, left, places = weights(blocks[at], members)
    cols = pl.ds(at * WIDTH, WIDTH)
    pa3 = stacked(pa)
    pa3_out[:, cols] = pa3
    left_out[:, cols] = left
    place_out[:, cols] = places
    return pa3, left, places


def add_blocks(members, acc, blocks, xt, meta, outs):
    rows_x = side(xt[:, :members])
    own_places = meta[...].T[:, TILE : TILE + 1]
    for at in range(blocks.shape[0]):
        pa3, left, places = weigh(blocks, at, members, *outs)
        left2 = jnp.concatenate(halves(left), axis=0)
        acc = add_block(acc, rows_x, pa3, left2, places, own_places)
    return acc


def half_kernel(members, blocks, xt_ref, meta, high, low, *outs):
    acc = zero_acc(WIDTH, members)
    high[...], low[...] = add_blocks(members, acc, blocks, xt_ref[...], meta, outs)


def next_kernel(members, blocks, xt_ref, meta, high, low, q_out, *outs):
    xt = xt_ref[...]
    acc = add_blocks(members, (high[...], low[...]), blocks, xt, meta, outs)
    pad = jnp.zeros((WIDTH, LANES - members), F32)
    new = xt + jnp.concatenate([summed(acc), pad], axis=1)
    q_out[pl.ds(0, members), :] = new.T[:members]
    q_out[pl.ds(members, 8), :] = meta[...]


def add_gram(members, tpd, info, parts, gram, total):
    m_dev = members // 2
    start = pl.multiple_of(info[1] * m_dev, 8)
    high_sum, low_sum = gram
    for pa3_ref, left_ref, place_ref in parts:
        for at in range(pa3_ref.shape[1] // WIDTH):
            cols = pl.ds(at * WIDTH, WIDTH)
            left = left_ref[pl.ds(start, m_dev), cols]
            places = place_ref[:, cols]
            scaled = [
                left * taper((info[0] + tile).astype(F32) * (2.0 / total), places)
                for tile in range(tpd)
            ]
            high, low = halves(jnp.concatenate(scaled, axis=0))
            pa3 = pa3_ref[:, cols]
            high_sum += nt_dot(high, pa3[members:])
            low_sum += nt_dot(low, pa3[:members])
    return high_sum, low_sum


def update_state(members, tpd, info, gram, own, other, new):
    m_dev = members // 2
    core = info[1]
    gram = side(summed(gram))
    n_part = own.shape[0] // (m_dev * tpd)
    for tile in range(tpd):
        rows = [pl.ds(part * m_dev * tpd + tile, m_dev, stride=tpd) for part in range(n_part)]
        a = jnp.concatenate([own[row, :] for row in rows], axis=1)
        b = jnp.concatenate([other[row, :] for row in rows], axis=1)
        whole = jnp.concatenate([jnp.where(core == 0, a, b), jnp.where(core == 0, b, a)], axis=0)
        got = a + nn_dot(gram[tile * m_dev : (tile + 1) * m_dev], stacked(whole))
        for part, row in enumerate(rows):
            new[row, :] = got[:, part * LANES : (part + 1) * LANES]


def later_kernel(members, total, tpd, info, *refs):
    parts, (own, other), refs = (refs[:3], refs[3:6]), refs[6:8], refs[8:]
    n_later = (len(refs) - 1) // 3
    xts, metas, outs = refs[:n_later], refs[n_later : 2 * n_later], refs[2 * n_later : -1]
    for xt_ref, meta, out in zip(xts, metas, outs):
        xt = xt_ref[...]
        rows_x = side(xt[:, :members])
        own_places = meta[...].T[:, TILE : TILE + 1]
        acc = zero_acc(WIDTH, members)
        for pa3_ref, left_ref, place_ref in parts:
            for at in range(pa3_ref.shape[1] // WIDTH):
                cols = pl.ds(at * WIDTH, WIDTH)
                left2 = jnp.concatenate(halves(left_ref[:, cols]), axis=0)
                acc = add_block(
                    acc, rows_x, pa3_ref[:, cols], left2, place_ref[:, cols], own_places
                )
        pad = jnp.zeros((WIDTH, LANES - members), F32)
        out[...] = xt + jnp.concatenate([summed(acc), pad], axis=1)
    gram = add_gram(members, tpd, info, parts, zero_acc(tpd * members // 2, members), total)
    update_state(members, tpd, info, gram, own, other, refs[-1])


def gram_kernel(members, total, tpd, info, blocks, high, low, *parts):
    for at in range(blocks.shape[0]):
        weigh(blocks, at, members, *parts)
    gram = zero_acc(tpd * members // 2, members)
    high[...], low[...] = add_gram(members, tpd, info, [parts], gram, total)


def last_kernel(members, total, tpd, info, blocks, high, low, own, other, out, new, *parts):
    for at in range(blocks.shape[0]):
        weigh(blocks, at, members, *parts)
    gram = add_gram(members, tpd, info, [parts], (high[...], low[...]), total)
    update_state(members, tpd, info, gram, own, other, new)
    rows = out.shape[0]
    for part in range(new.shape[0] // rows):
        out[:, pl.ds(part * LANES, LANES)] = new[pl.ds(part * rows, rows), :]


def vmem(n):
    return [pl.BlockSpec(memory_space=pltpu.VMEM)] * n


def smem(n):
    return [pl.BlockSpec(memory_space=pltpu.SMEM)] * n


def out_f32(*shape):
    return jax.ShapeDtypeStruct(shape, F32)


def ring(n, shift):
    return [(i, (i + shift) % n) for i in range(n)]


def call(kernel, name, n_smem, n_vmem, outs, flops, scratch=(), out_specs=None):
    return pl.pallas_call(
        kernel,
        out_shape=outs,
        in_specs=smem(n_smem) + vmem(n_vmem),
        out_specs=out_specs or (vmem(len(outs)) if isinstance(outs, list) else vmem(1)[0]),
        scratch_shapes=list(scratch),
        compiler_params=pltpu.CompilerParams(vmem_limit_bytes=24 * MIB),
        cost_estimate=pl.CostEstimate(flops=flops, bytes_accessed=4 * MIB, transcendentals=0),
        name=name,
    )


def per_device(ensemble, obs_cell, obs_value, obs_var):
    m_dev, tpd, points = ensemble.shape
    n_tile = lax.axis_size("tile")
    n_obs = lax.axis_size("obs")
    members = 2 * m_dev
    per_dev = obs_cell.shape[1]
    half = per_dev // 2
    part = half // n_obs
    batch_obs = per_dev * n_tile
    height = members + 8
    total = tpd * n_tile * n_obs
    slab_cells = tpd * points
    tile_at, obs_at, core = (lax.axis_index(a) for a in ("tile", "obs", "mem"))
    first_tile = (tile_at * n_obs + obs_at) * tpd
    info = jnp.stack([first_tile, core, obs_at, tile_at]).astype(jnp.int32)
    swap = functools.partial(lax.ppermute, axis_name="mem", perm=[(0, 1), (1, 0)])

    def shifted(x):
        return [x] + [lax.ppermute(x, "obs", ring(n_obs, k)) for k in range(1, n_obs)]

    def own_half(x):
        return lax.dynamic_slice(x, (0, core * half), (1, half))

    kind = lax.broadcasted_iota(jnp.int32, (4, half), 0)
    packed = jnp.where(kind == 1, own_half(obs_value), own_half(obs_var))
    packed = jnp.where(kind == 0, own_half(obs_cell).astype(F32), packed)
    near = shifted(packed)
    flat = (m_dev * tpd * points // LANES, LANES)
    split = call(split_kernel, "split", 0, 1, out_f32(*flat), 10**6)
    state = split(ensemble.reshape(m_dev * tpd, points))
    chunks = shifted(state)
    others = [swap(chunk) for chunk in chunks]
    mix = functools.partial(mix_kernel, part)
    sent = call(mix, "mix", 1, n_obs, out_f32(n_tile, 1, 4 * half), 10**10)(info, *near)
    lists = lax.all_to_all(sent, "tile", 0, 0)
    n_rows = n_tile * half
    found = call(
        functools.partial(find_kernel, n_obs, slab_cells, half),
        "find",
        1,
        1,
        jax.ShapeDtypeStruct((n_tile, LANES), jnp.int32),
        10**10,
    )(info, lists)
    most_sends = -(-n_rows // ROOM)
    first, held = call(
        functools.partial(pick_kernel, n_obs, m_dev, tpd, half),
        "pick",
        2,
        2 * n_obs,
        [out_f32(n_tile, SENT, LANES), out_f32(most_sends * ROOM, LANES)],
        10**9,
        [
            pltpu.VMEM((n_obs * slab_cells, LANES), F32),
        ],
    )(info, found, *chunks, *others)
    first, lists = lax.optimization_barrier((first, lists))
    cells = lists[:, 0, :half].reshape(n_rows).astype(jnp.int32)
    owner = cells // (slab_cells * n_obs)
    ints = [jax.ShapeDtypeStruct((n,), jnp.int32) for n in (n_rows, n_rows, 1)]
    source, ranks, rounds = call(
        functools.partial(place_kernel, n_tile),
        "place",
        1,
        0,
        ints,
        10**9,
        [pltpu.SMEM((n_tile,), jnp.int32)],
        smem(3),
    )(owner)
    lists = jnp.transpose(lists.reshape(n_tile, 4, n_obs, part), (2, 1, 0, 3))
    lists = lists.reshape(n_obs, 4, WIDTH)
    metas = []
    for batch in range(n_obs):
        at = (obs_at - batch + n_obs) % n_obs
        one = lax.dynamic_slice(lists, (at, 0, 0), (1, 4, WIDTH))[0]
        place = (one[:1].astype(jnp.int32) // points).astype(F32) * (2.0 / total)
        metas.append(jnp.concatenate([one[1:3], place, jnp.zeros((5, WIDTH), F32)], axis=0))

    space = [pltpu.VMEM((n_tile * ROOM + n_rows, LANES), F32)]
    got = lax.all_to_all(first, "tile", 0, 0)

    def again(at, late):
        more = lax.dynamic_slice(held, (at * ROOM, 0), (ROOM, LANES))
        repack = functools.partial(repack_kernel, members)
        more = call(repack, "repack", 0, 1, out_f32(n_tile, SENT, LANES), 10**6)(more)
        got = lax.all_to_all(more, "tile", 0, 0)
        rest = functools.partial(rest_kernel, members)
        return call(rest, "rest", 3, 2, out_f32(n_rows, LANES), 10**8, space)(
            at.reshape(1), owner, ranks, got, late
        )

    got, late = lax.optimization_barrier((got, jnp.zeros((n_rows, LANES), F32)))
    late = lax.fori_loop(jnp.int32(1), rounds[0], again, late)
    q = call(
        functools.partial(first_kernel, members, n_obs, part),
        "first",
        2,
        3,
        out_f32(height, WIDTH),
        10**8,
        space + [pltpu.VMEM((WIDTH, LANES), F32)],
    )(info, source, got, late, metas[0])
    xts = call(
        functools.partial(others_kernel, members, n_obs, part),
        "others",
        2,
        2,
        [out_f32(WIDTH, LANES)] * (n_obs - 1),
        8 * 10**9,
        space,
    )(info, source, got, late)
    metas = metas[1:]
    own4 = jnp.stack(shifted(q))
    own4, xts = lax.optimization_barrier((own4, xts))
    oth4 = swap(own4)


    other = others[0]
    n_half = batch_obs // 2
    weighed = [
        jax.ShapeDtypeStruct((3 * members, n_half), BF16),
        out_f32(members, n_half),
        out_f32(1, n_half),
    ]
    space = [pltpu.VMEM(x.shape, x.dtype) for x in weighed]
    rows = tpd * m_dev
    for batch in range(n_obs - 1):
        xt, xts, meta, metas = xts[0], xts[1:], metas[0], metas[1:]
        sums = [out_f32(WIDTH, 2 * members), out_f32(WIDTH, members)]
        high, low, *part_a = call(
            functools.partial(half_kernel, members), f"half{batch}", 0, 3, sums + weighed, 10**9
        )(own4, xt, meta)
        q, *part_b = call(
            functools.partial(next_kernel, members),
            f"next{batch}",
            0,
            5,
            [out_f32(height, WIDTH)] + weighed,
            10**9,
        )(oth4, xt, meta, high, low)
        own4 = jnp.stack(shifted(q))
        *xts, state = call(
            functools.partial(later_kernel, members, total, tpd),
            f"later{batch}",
            1,
            8 + 2 * len(xts),
            [out_f32(WIDTH, LANES)] * len(xts) + [out_f32(*state.shape)],
            8 * 10**9,
        )(info, *part_a, *part_b, state, other, *xts, *metas)
        own4, state = lax.optimization_barrier((own4, state))
        oth4, other = swap(own4), swap(state)
    high, low = call(
        functools.partial(gram_kernel, members, total, tpd),
        "gram",
        1,
        1,
        [out_f32(rows, 2 * members), out_f32(rows, members)],
        2 * 10**9,
        space,
    )(info, own4)
    state = call(
        functools.partial(last_kernel, members, total, tpd),
        "last",
        1,
        5,
        out_f32(m_dev * tpd, points),
        2 * 10**9,
        [pltpu.VMEM(state.shape, F32)] + space,
    )(info, oth4, high, low, state, other)
    return state.reshape(m_dev, tpd, points)


def solution(mesh):
    return jax.shard_map(
        per_device,
        mesh=mesh,
        in_specs=(
            P("mem", ("tile", "obs"), None),
            P("obs", "tile"),
            P("obs", "tile"),
            P("obs", "tile"),
        ),
        out_specs=P("mem", ("tile", "obs"), None),
        check_vma=False,
    )
```

```python
import functools

import jax
import jax.numpy as jnp
from jax import lax
from jax.experimental import pallas as pl
from jax.experimental.pallas import tpu as pltpu
from jax.sharding import PartitionSpec as P

LANES = 128
WIDTH = 256
ROOM, SENT = 56, 40
VALUE, VAR, TILE = 0, 1, 2
MIB = 1024 * 1024
F32, BF16 = jnp.float32, jnp.bfloat16


def halves(x):
    high = x.astype(BF16)
    return high, (x - high.astype(F32)).astype(BF16)


def nn_dot(a, b):
    return jnp.dot(a, b, preferred_element_type=F32)


def nt_dot(a, b):
    return lax.dot_general(a, b, (((1,), (1,)), ((), ())), preferred_element_type=F32)


def taper(place_a, place_b):
    delta = jnp.abs(place_a - place_b)
    z = jnp.minimum(delta, 2.0 - delta)
    return (((-0.25 * z + 0.5) * z + 0.625) * z - 5.0 / 3.0) * (z * z) + 1.0


def side(x):
    high, low = halves(x)
    return jnp.concatenate([high.astype(F32), low.astype(F32), high.astype(F32)], axis=1).astype(BF16)


def stacked(x):
    high, low = halves(x)
    return jnp.concatenate([high, high, low], axis=0)


def split_kernel(state, out):
    rows, points = state.shape
    for part in range(points // LANES):
        out[pl.ds(part * rows, rows), :] = state[:, pl.ds(part * LANES, LANES)]


def here(total=0):
    tile_at, obs_at, core = (lax.axis_index(a) for a in ("tile", "obs", "mem"))
    n_obs = lax.axis_size("obs")
    slab = tile_at * n_obs + obs_at
    return slab * (total // (lax.axis_size("tile") * n_obs)), core, obs_at, tile_at


def mix_kernel(part, *refs):
    info = here()
    lists, out = refs[:-1], refs[-1]
    fields, width = lists[0].shape
    lane = lax.broadcasted_iota(jnp.int32, (8, LANES), 1)
    mixed = jnp.zeros((8, LANES), F32)
    for at, ref in enumerate(lists):
        wide = jnp.concatenate([ref[...], jnp.zeros((fields, LANES - width), F32)], axis=1)
        wide = jnp.concatenate([wide, jnp.zeros((8 - fields, LANES), F32)], axis=0)
        moved = pltpu.roll(wide, lax.rem(LANES + (at - info[2]) * part, LANES), 1)
        mixed = jnp.where((lane >= at * part) & (lane < (at + 1) * part), moved, mixed)
    row = mixed[:1]
    for field in range(1, fields):
        row = row + pltpu.roll(mixed, field * width, 1)[field : field + 1]
    for who in range(out.shape[0]):
        out[who] = row


def find_kernel(n_src, slab_cells, half, lists, found):
    info = here()
    n_tile = lists.shape[0]
    cells = jnp.concatenate([lists[who] for who in range(n_tile)], axis=0).astype(jnp.int32)
    slab = lax.shift_right_logical(cells, slab_cells.bit_length() - 1)
    owner = lax.shift_right_logical(slab, n_src.bit_length() - 1)
    place = (info[2] - (slab & (n_src - 1)) + n_src) & (n_src - 1)
    lane = lax.broadcasted_iota(jnp.int32, cells.shape, 1)
    bits = jnp.where((owner == info[3]) & (lane < half), lax.shift_left(1, 15 - (lane & 15)), 0)
    bits = bits.astype(F32)
    upper = jnp.sum(jnp.where(lane < 16, bits, 0.0), axis=1, keepdims=True).astype(jnp.int32)
    lower = jnp.sum(jnp.where(lane >= 16, bits, 0.0), axis=1, keepdims=True).astype(jnp.int32)
    mask = lax.shift_left(upper, 16) | lower
    found[...] = jnp.where(lane < half, place * slab_cells + (cells & (slab_cells - 1)), mask)


def pick_kernel(n_src, m_dev, tpd, half, rows_at, *refs):
    info = here()
    chunks, (sent, out, cols) = refs[: 2 * n_src], refs[2 * n_src :]
    core = info[1]
    members = 2 * m_dev
    n_part = chunks[0].shape[0] // (m_dev * tpd)
    points = n_part * LANES
    for src in range(n_src):
        for part in range(n_part):
            for tile in range(tpd):
                rows = pl.ds(part * m_dev * tpd + tile, m_dev, stride=tpd)
                a, b = chunks[src][rows, :], chunks[n_src + src][rows, :]
                block = jnp.concatenate(
                    [
                        jnp.where(core == 0, a, b),
                        jnp.where(core == 0, b, a),
                        jnp.zeros((LANES - members, LANES), F32),
                    ],
                    axis=0,
                )
                start = (src * tpd + tile) * points + part * LANES
                cols[pl.ds(start, LANES), :] = block.T

    def one_tile(tile, rank):
        def one_row(carry):
            mask, rank = carry
            at = lax.clz(mask)
            out[pl.ds(rank, 1), :] = cols[pl.ds(rows_at[tile, at], 1), :]
            return mask ^ lax.shift_left(jnp.int32(1), 31 - at), rank + 1

        start = (rows_at[tile, half], rank)
        return lax.while_loop(lambda carry: carry[0] != 0, one_row, start)[1]

    lax.fori_loop(0, rows_at.shape[0], one_tile, jnp.int32(0))
    pack_rows(out, sent, members)


def pack_rows(rows, sent, members):
    packed = [rows[pl.ds(8 * at, 8), :] for at in range(SENT // 8)]
    spare = lax.broadcasted_iota(jnp.int32, (8, LANES), 1) >= members
    for at in range((ROOM - SENT) // 8):
        tail = rows[pl.ds(SENT + 8 * at, 8), :]
        for half, shift in enumerate((members, 2 * members - LANES)):
            here = 2 * at + half
            packed[here] = jnp.where(spare, pltpu.roll(tail, shift, 1), packed[here])
    for who in range(sent.shape[0]):
        for at, block in enumerate(packed):
            sent[who, pl.ds(8 * at, 8), :] = block


def unpack_rows(sent, rows, members):
    split = LANES - members
    lane = lax.broadcasted_iota(jnp.int32, (8, LANES), 1)
    for who in range(sent.shape[0]):
        rows[pl.ds(who * ROOM, SENT), :] = sent[who]
        for at in range((ROOM - SENT) // 8):
            one = pltpu.roll(sent[who, pl.ds(16 * at, 8), :], split, 1)
            two = pltpu.roll(sent[who, pl.ds(16 * at + 8, 8), :], 2 * split, 1)
            rows[pl.ds(who * ROOM + SENT + 8 * at, 8), :] = jnp.where(lane < split, one, two)


def repack_kernel(members, held, out):
    pack_rows(held, out, members)


def place_kernel(n_tile, owner, source, ranks, rounds, count):
    for at in range(n_tile):
        count[at] = 0

    def body(step, most):
        for part in range(8):
            row = step * 8 + part
            who = owner[row]
            rank = count[who]
            count[who] = rank + 1
            ranks[row] = rank
            source[row] = jnp.where(rank < ROOM, who * ROOM + rank, n_tile * ROOM + row)
            most = jnp.maximum(most, rank)
        return most

    rounds[0] = lax.fori_loop(0, owner.shape[0] // 8, body, jnp.int32(0)) // ROOM + 1


def rest_kernel(members, at, owner, ranks, sent, before, late, got):
    unpack_rows(sent, got, members)
    late[...] = before[...]

    def body(row, carry):
        rank = ranks[row] - at[0] * ROOM

        @pl.when((rank >= 0) & (rank < ROOM))
        def _():
            late[pl.ds(row, 1), :] = got[pl.ds(owner[row] * ROOM + rank, 1), :]

        return carry

    lax.fori_loop(0, late.shape[0], body, 0)


def take_rows(members, n_obs, part, batches, source, sent, late, outs, got):
    info = here()
    unpack_rows(sent, got, members)
    n_tile = sent.shape[0]
    got[pl.ds(n_tile * ROOM, late.shape[0]), :] = late[...]
    near = [lax.rem(info[2] - batch + n_obs, n_obs) for batch in batches]

    def body(step, carry):
        for half in range(2):
            who = step * 2 + half
            base = pl.multiple_of(step * 2 * part, 2 * part)
            for place, out in zip(near, outs):
                first = (who * n_obs + place) * part
                for row in range(part):
                    at = source[first + row]
                    out[pl.ds(base + half * part + row, 1), :] = got[pl.ds(at, 1), :]
        return carry

    lax.fori_loop(0, n_tile // 2, body, 0)


def first_kernel(members, n_obs, part, source, sent, late, meta, q, got, rows):
    take_rows(members, n_obs, part, [0], source, sent, late, [rows], got)
    q[pl.ds(0, members), :] = rows[...].T[:members]
    q[pl.ds(members, 8), :] = meta[...]


def others_kernel(members, n_obs, part, source, sent, late, *refs):
    take_rows(
        members, n_obs, part, range(1, n_obs), source, sent, late, refs[:-1], refs[-1]
    )


def weights(block, members):
    x = block[:members]
    mean = jnp.sum(x, axis=0, keepdims=True) / members
    pa = x - mean
    value = block[members + VALUE : members + VALUE + 1]
    var = block[members + VAR : members + VAR + 1]
    places = block[members + TILE : members + TILE + 1]
    total_var = jnp.sum(pa * pa, axis=0, keepdims=True) / (members - 1) + var
    alpha = 1.0 / (1.0 + jnp.sqrt(var / total_var))
    weight_a = alpha / total_var
    weight_d = (value - mean) / total_var
    left = (weight_d - weight_a * pa) / (members - 1)
    return pa, left, places


def add_block(acc, rows_x, pa3, left2, places, own_places):
    members = left2.shape[0] // 2
    high, low = halves(taper(own_places, places) * nn_dot(rows_x, pa3))
    return acc[0] + nt_dot(high, left2), acc[1] + nt_dot(low, left2[:members])


def zero_acc(n, members):
    return jnp.zeros((n, 2 * members), F32), jnp.zeros((n, members), F32)


def summed(acc):
    members = acc[1].shape[1]
    return acc[0][:, :members] + acc[0][:, members:] + acc[1]


def weigh(blocks, at, members, pa3_out, left_out, place_out):
    pa, left, places = weights(blocks[at], members)
    cols = pl.ds(at * WIDTH, WIDTH)
    pa3 = stacked(pa)
    pa3_out[:, cols] = pa3
    left_out[:, cols] = left
    place_out[:, cols] = places
    return pa3, left, places


def add_blocks(members, acc, blocks, xt, meta, outs):
    rows_x = side(xt[:, :members])
    own_places = meta[...].T[:, TILE : TILE + 1]
    for at in range(blocks.shape[0]):
        pa3, left, places = weigh(blocks, at, members, *outs)
        left2 = jnp.concatenate(halves(left), axis=0)
        acc = add_block(acc, rows_x, pa3, left2, places, own_places)
    return acc


def half_kernel(members, blocks, xt_ref, meta, high, low, *outs):
    acc = zero_acc(WIDTH, members)
    high[...], low[...] = add_blocks(members, acc, blocks, xt_ref[...], meta, outs)


def next_kernel(members, blocks, xt_ref, meta, high, low, q_out, *outs):
    xt = xt_ref[...]
    acc = add_blocks(members, (high[...], low[...]), blocks, xt, meta, outs)
    pad = jnp.zeros((WIDTH, LANES - members), F32)
    new = xt + jnp.concatenate([summed(acc), pad], axis=1)
    q_out[pl.ds(0, members), :] = new.T[:members]
    q_out[pl.ds(members, 8), :] = meta[...]


def add_gram(tiles, start, count, parts, gram, total):
    high_sum, low_sum = gram
    members = low_sum.shape[1]
    for pa3_ref, left_ref, place_ref in parts:
        for at in range(pa3_ref.shape[1] // WIDTH):
            cols = pl.ds(at * WIDTH, WIDTH)
            left = left_ref[pl.ds(start, count), cols]
            places = place_ref[:, cols]
            scaled = [left * taper(t.astype(F32) * (2.0 / total), places) for t in tiles]
            high, low = halves(jnp.concatenate(scaled, axis=0))
            pa3 = pa3_ref[:, cols]
            high_sum += nt_dot(high, pa3[members:])
            low_sum += nt_dot(low, pa3[:members])
    return high_sum, low_sum


def own_gram(members, tpd, info, parts, gram, total):
    start = pl.multiple_of(info[1] * (members // 2), 8)
    tiles = [info[0] + tile for tile in range(tpd)]
    return add_gram(tiles, start, members // 2, parts, gram, total)


def tiles_kernel(m_dev, tpd, own, other, tiles):
    info = here()
    core = info[1]
    n_half = tpd // 2
    for at in range(n_half):
        for part in range(own.shape[0] // (m_dev * tpd)):
            first = part * m_dev * tpd + at
            low, high = (pl.ds(first + n, m_dev, stride=tpd) for n in (0, n_half))
            a = jnp.where(core == 0, own[low, :], own[high, :])
            b = jnp.where(core == 0, other[low, :], other[high, :])
            whole = [jnp.where(core == 0, a, b), jnp.where(core == 0, b, a)]
            tiles[at, :, pl.ds(part * LANES, LANES)] = jnp.concatenate(whole, axis=0)


def later_kernel(members, total, n_later, n_state, *refs):
    info = here(total)
    refs = list(refs)
    take = lambda n: [refs.pop(0) for _ in range(n)]
    parts = [take(3), take(3)] if n_later else []
    xts, metas = take(n_later), take(n_later)
    batches = [[take(3), take(3)] for _ in range(n_state)]
    state = take(1)[0] if n_state else None
    for xt_ref, meta in zip(xts, metas):
        xt = xt_ref[...]
        rows_x = side(xt[:, :members])
        own_places = meta[...].T[:, TILE : TILE + 1]
        acc = zero_acc(WIDTH, members)
        for pa3_ref, left_ref, place_ref in parts:
            for at in range(pa3_ref.shape[1] // WIDTH):
                cols = pl.ds(at * WIDTH, WIDTH)
                left2 = jnp.concatenate(halves(left_ref[:, cols]), axis=0)
                acc = add_block(
                    acc, rows_x, pa3_ref[:, cols], left2, place_ref[:, cols], own_places
                )
        pad = jnp.zeros((WIDTH, LANES - members), F32)
        take(1)[0][...] = xt + jnp.concatenate([summed(acc), pad], axis=1)
    for which, sets in enumerate(batches):
        new = refs[0]
        n_tile = new.shape[0]
        tiles = [info[0] + info[1] * n_tile + at for at in range(n_tile)]
        gram = add_gram(tiles, 0, members, sets, zero_acc(n_tile * members, members), total)
        gram = side(summed(gram))
        for at in range(n_tile):
            whole = (new if which else state)[at]
            new[at] = whole + nn_dot(gram[at * members : (at + 1) * members], stacked(whole))


def gram_kernel(members, total, tpd, blocks, high, low, *parts):
    info = here(total)
    for at in range(blocks.shape[0]):
        weigh(blocks, at, members, *parts)
    gram = zero_acc(tpd * members // 2, members)
    high[...], low[...] = own_gram(members, tpd, info, [parts], gram, total)


def last_kernel(members, total, tpd, blocks, high, low, mine, other, out, new, *parts):
    info = here(total)
    for at in range(blocks.shape[0]):
        weigh(blocks, at, members, *parts)
    gram = own_gram(members, tpd, info, [parts], (high[...], low[...]), total)
    gram = side(summed(gram))
    m_dev, core = members // 2, info[1]
    n_half = mine.shape[0]
    for tile in range(tpd):
        at = tile % n_half
        whole = jnp.where(core == tile // n_half, mine[at], other[at])
        got = jnp.where(core == 0, whole[:m_dev], whole[m_dev:])
        got = got + nn_dot(gram[tile * m_dev : (tile + 1) * m_dev], stacked(whole))
        for part in range(got.shape[1] // LANES):
            row = pl.ds(part * m_dev * tpd + tile, m_dev, stride=tpd)
            new[row, :] = got[:, part * LANES : (part + 1) * LANES]
    rows = out.shape[0]
    for part in range(new.shape[0] // rows):
        out[:, pl.ds(part * LANES, LANES)] = new[pl.ds(part * rows, rows), :]


def vmem(n):
    return [pl.BlockSpec(memory_space=pltpu.VMEM)] * n


def smem(n):
    return [pl.BlockSpec(memory_space=pltpu.SMEM)] * n


def out_f32(*shape):
    return jax.ShapeDtypeStruct(shape, F32)


def ring(n, shift):
    return [(i, (i + shift) % n) for i in range(n)]


def call(kernel, name, n_smem, n_vmem, outs, flops, scratch=(), out_specs=None):
    return pl.pallas_call(
        kernel,
        out_shape=outs,
        in_specs=smem(n_smem) + vmem(n_vmem),
        out_specs=out_specs or (vmem(len(outs)) if isinstance(outs, list) else vmem(1)[0]),
        scratch_shapes=list(scratch),
        compiler_params=pltpu.CompilerParams(vmem_limit_bytes=24 * MIB),
        cost_estimate=pl.CostEstimate(flops=flops, bytes_accessed=4 * MIB, transcendentals=0),
        name=name,
    )


def per_device(ensemble, obs_cell, obs_value, obs_var):
    m_dev, tpd, points = ensemble.shape
    n_tile = lax.axis_size("tile")
    n_obs = lax.axis_size("obs")
    members = 2 * m_dev
    per_dev = obs_cell.shape[1]
    half = per_dev // 2
    part = half // n_obs
    batch_obs = per_dev * n_tile
    height = members + 8
    total = tpd * n_tile * n_obs
    slab_cells = tpd * points
    tile_at, obs_at, core = (lax.axis_index(a) for a in ("tile", "obs", "mem"))
    swap = functools.partial(lax.ppermute, axis_name="mem", perm=[(0, 1), (1, 0)])

    def shifted(x):
        return [x] + [lax.ppermute(x, "obs", ring(n_obs, k)) for k in range(1, n_obs)]

    def own_half(x):
        return lax.dynamic_slice(x, (0, core * half), (1, half))

    kind = lax.broadcasted_iota(jnp.int32, (4, half), 0)
    packed = jnp.where(kind == 1, own_half(obs_value), own_half(obs_var))
    packed = jnp.where(kind == 0, own_half(obs_cell).astype(F32), packed)
    near = shifted(packed)
    flat = (m_dev * tpd * points // LANES, LANES)
    split = call(split_kernel, "split", 0, 1, out_f32(*flat), 10**6)
    state = split(ensemble.reshape(m_dev * tpd, points))
    chunks = shifted(state)
    others = [swap(chunk) for chunk in chunks]
    mix = functools.partial(mix_kernel, part)
    sent = call(mix, "mix", 0, n_obs, out_f32(n_tile, 1, 4 * half), 10**10)(*near)
    lists = lax.all_to_all(sent, "tile", 0, 0)
    n_rows = n_tile * half
    found = call(
        functools.partial(find_kernel, n_obs, slab_cells, half),
        "find",
        0,
        1,
        jax.ShapeDtypeStruct((n_tile, LANES), jnp.int32),
        10**10,
    )(lists)
    most_sends = -(-n_rows // ROOM)
    first, held = call(
        functools.partial(pick_kernel, n_obs, m_dev, tpd, half),
        "pick",
        1,
        2 * n_obs,
        [out_f32(n_tile, SENT, LANES), out_f32(most_sends * ROOM, LANES)],
        10**9,
        [
            pltpu.VMEM((n_obs * slab_cells, LANES), F32),
        ],
    )(found, *chunks, *others)
    first, lists = lax.optimization_barrier((first, lists))
    cells = lists[:, 0, :half].reshape(n_rows).astype(jnp.int32)
    owner = cells // (slab_cells * n_obs)
    ints = [jax.ShapeDtypeStruct((n,), jnp.int32) for n in (n_rows, n_rows, 1)]
    source, ranks, rounds = call(
        functools.partial(place_kernel, n_tile),
        "place",
        1,
        0,
        ints,
        10**9,
        [pltpu.SMEM((n_tile,), jnp.int32)],
        smem(3),
    )(owner)
    lists = jnp.transpose(lists.reshape(n_tile, 4, n_obs, part), (2, 1, 0, 3))
    lists = lists.reshape(n_obs, 4, WIDTH)
    metas = []
    for batch in range(n_obs):
        at = (obs_at - batch + n_obs) % n_obs
        one = lax.dynamic_slice(lists, (at, 0, 0), (1, 4, WIDTH))[0]
        place = (one[:1].astype(jnp.int32) // points).astype(F32) * (2.0 / total)
        metas.append(jnp.concatenate([one[1:3], place, jnp.zeros((5, WIDTH), F32)], axis=0))

    space = [pltpu.VMEM((n_tile * ROOM + n_rows, LANES), F32)]
    got = lax.all_to_all(first, "tile", 0, 0)

    def again(at, late):
        more = lax.dynamic_slice(held, (at * ROOM, 0), (ROOM, LANES))
        repack = functools.partial(repack_kernel, members)
        more = call(repack, "repack", 0, 1, out_f32(n_tile, SENT, LANES), 10**6)(more)
        got = lax.all_to_all(more, "tile", 0, 0)
        rest = functools.partial(rest_kernel, members)
        return call(rest, "rest", 3, 2, out_f32(n_rows, LANES), 10**8, space)(
            at.reshape(1), owner, ranks, got, late
        )

    got, late = lax.optimization_barrier((got, jnp.zeros((n_rows, LANES), F32)))
    late = lax.fori_loop(jnp.int32(1), rounds[0], again, late)
    q = call(
        functools.partial(first_kernel, members, n_obs, part),
        "first",
        1,
        3,
        out_f32(height, WIDTH),
        10**8,
        space + [pltpu.VMEM((WIDTH, LANES), F32)],
    )(source, got, late, metas[0])
    xts = call(
        functools.partial(others_kernel, members, n_obs, part),
        "others",
        1,
        2,
        [out_f32(WIDTH, LANES)] * (n_obs - 1),
        8 * 10**9,
        space,
    )(source, got, late)
    metas = metas[1:]
    own4 = jnp.stack(shifted(q))
    tiles = call(
        functools.partial(tiles_kernel, m_dev, tpd),
        "tiles",
        0,
        2,
        out_f32(tpd // 2, members, points),
        10**7,
    )(state, others[0])
    own4, xts, tiles = lax.optimization_barrier((own4, xts, tiles))
    oth4 = swap(own4)


    n_half = batch_obs // 2
    weighed = [
        jax.ShapeDtypeStruct((3 * members, n_half), BF16),
        out_f32(members, n_half),
        out_f32(1, n_half),
    ]
    space = [pltpu.VMEM(x.shape, x.dtype) for x in weighed]
    rows = tpd * m_dev
    parts = {}
    for batch in range(n_obs - 1):
        xt, xts, meta, metas = xts[0], xts[1:], metas[0], metas[1:]
        sums = [out_f32(WIDTH, 2 * members), out_f32(WIDTH, members)]
        high, low, *part_a = call(
            functools.partial(half_kernel, members), f"half{batch}", 0, 3, sums + weighed, 10**9
        )(own4, xt, meta)
        q, *part_b = call(
            functools.partial(next_kernel, members),
            f"next{batch}",
            0,
            5,
            [out_f32(height, WIDTH)] + weighed,
            10**9,
        )(oth4, xt, meta, high, low)
        own4 = jnp.stack(shifted(q))
        parts[batch] = part_a + part_b
        due = [[], [0], [1, 2]][batch]
        if xts:
            work = parts[batch] + list(xts) + metas
        else:
            work = []
        work += sum([parts[at] for at in due], []) + ([tiles] if due else [])
        outs = [out_f32(WIDTH, LANES)] * len(xts) + [out_f32(*tiles.shape)] * bool(due)
        done = call(
            functools.partial(later_kernel, members, total, len(xts), len(due)),
            f"later{batch}",
            0,
            len(work),
            outs,
            8 * 10**9,
        )(*work)
        own4, done = lax.optimization_barrier((own4, done))
        xts, tiles = list(done[: len(xts)]), done[-1] if due else tiles
        oth4 = swap(own4)
    other = swap(tiles)
    high, low = call(
        functools.partial(gram_kernel, members, total, tpd),
        "gram",
        0,
        1,
        [out_f32(rows, 2 * members), out_f32(rows, members)],
        2 * 10**9,
        space,
    )(own4)
    state = call(
        functools.partial(last_kernel, members, total, tpd),
        "last",
        0,
        5,
        out_f32(m_dev * tpd, points),
        2 * 10**9,
        [pltpu.VMEM(state.shape, F32)] + space,
    )(oth4, high, low, tiles, other)
    return state.reshape(m_dev, tpd, points)


def solution(mesh):
    return jax.shard_map(
        per_device,
        mesh=mesh,
        in_specs=(
            P("mem", ("tile", "obs"), None),
            P("obs", "tile"),
            P("obs", "tile"),
            P("obs", "tile"),
        ),
        out_specs=P("mem", ("tile", "obs"), None),
        check_vma=False,
    )
```

```python
import functools

import jax
import jax.numpy as jnp
from jax import lax
from jax.experimental import pallas as pl
from jax.experimental.pallas import tpu as pltpu
from jax.sharding import PartitionSpec as P

LANES = 128
WIDTH = 256
ROOM, SENT = 56, 40
VALUE, VAR, TILE = 0, 1, 2
MIB = 1024 * 1024
F32, BF16 = jnp.float32, jnp.bfloat16


def halves(x):
    high = x.astype(BF16)
    return high, (x - high.astype(F32)).astype(BF16)


def nn_dot(a, b):
    return jnp.dot(a, b, preferred_element_type=F32)


def nt_dot(a, b):
    return lax.dot_general(a, b, (((1,), (1,)), ((), ())), preferred_element_type=F32)


def taper(place_a, place_b):
    delta = jnp.abs(place_a - place_b)
    z = jnp.minimum(delta, 2.0 - delta)
    return (((-0.25 * z + 0.5) * z + 0.625) * z - 5.0 / 3.0) * (z * z) + 1.0


def side(x):
    high, low = halves(x)
    return jnp.concatenate([high.astype(F32), low.astype(F32), high.astype(F32)], axis=1).astype(BF16)


def stacked(x):
    high, low = halves(x)
    return jnp.concatenate([high, high, low], axis=0)


def split_kernel(state, out):
    rows, points = state.shape
    for part in range(points // LANES):
        out[pl.ds(part * rows, rows), :] = state[:, pl.ds(part * LANES, LANES)]


def here(total=0):
    tile_at, obs_at, core = (lax.axis_index(a) for a in ("tile", "obs", "mem"))
    n_obs = lax.axis_size("obs")
    slab = tile_at * n_obs + obs_at
    return slab * (total // (lax.axis_size("tile") * n_obs)), core, obs_at, tile_at


def mix_kernel(part, *refs):
    info = here()
    lists, out = refs[:-1], refs[-1]
    fields, width = lists[0].shape
    lane = lax.broadcasted_iota(jnp.int32, (8, LANES), 1)
    mixed = jnp.zeros((8, LANES), F32)
    for at, ref in enumerate(lists):
        wide = jnp.concatenate([ref[...], jnp.zeros((fields, LANES - width), F32)], axis=1)
        wide = jnp.concatenate([wide, jnp.zeros((8 - fields, LANES), F32)], axis=0)
        moved = pltpu.roll(wide, lax.rem(LANES + (at - info[2]) * part, LANES), 1)
        mixed = jnp.where((lane >= at * part) & (lane < (at + 1) * part), moved, mixed)
    row = mixed[:1]
    for field in range(1, fields):
        row = row + pltpu.roll(mixed, field * width, 1)[field : field + 1]
    for who in range(out.shape[0]):
        out[who] = row


def find_kernel(n_src, slab_cells, half, lists, found):
    info = here()
    n_tile = lists.shape[0]
    cells = jnp.concatenate([lists[who] for who in range(n_tile)], axis=0).astype(jnp.int32)
    slab = lax.shift_right_logical(cells, slab_cells.bit_length() - 1)
    owner = lax.shift_right_logical(slab, n_src.bit_length() - 1)
    place = (info[2] - (slab & (n_src - 1)) + n_src) & (n_src - 1)
    lane = lax.broadcasted_iota(jnp.int32, cells.shape, 1)
    bits = jnp.where((owner == info[3]) & (lane < half), lax.shift_left(1, 15 - (lane & 15)), 0)
    bits = bits.astype(F32)
    upper = jnp.sum(jnp.where(lane < 16, bits, 0.0), axis=1, keepdims=True).astype(jnp.int32)
    lower = jnp.sum(jnp.where(lane >= 16, bits, 0.0), axis=1, keepdims=True).astype(jnp.int32)
    mask = lax.shift_left(upper, 16) | lower
    found[...] = jnp.where(lane < half, place * slab_cells + (cells & (slab_cells - 1)), mask)


def pick_kernel(n_src, m_dev, tpd, half, rows_at, *refs):
    info = here()
    chunks, (sent, out, cols) = refs[: 2 * n_src], refs[2 * n_src :]
    core = info[1]
    members = 2 * m_dev
    n_part = chunks[0].shape[0] // (m_dev * tpd)
    points = n_part * LANES
    for src in range(n_src):
        for part in range(n_part):
            for tile in range(tpd):
                rows = pl.ds(part * m_dev * tpd + tile, m_dev, stride=tpd)
                a, b = chunks[src][rows, :], chunks[n_src + src][rows, :]
                block = jnp.concatenate(
                    [
                        jnp.where(core == 0, a, b),
                        jnp.where(core == 0, b, a),
                        jnp.zeros((LANES - members, LANES), F32),
                    ],
                    axis=0,
                )
                start = (src * tpd + tile) * points + part * LANES
                cols[pl.ds(start, LANES), :] = block.T

    def one_tile(tile, rank):
        def one_row(carry):
            mask, rank = carry
            at = lax.clz(mask)
            out[pl.ds(rank, 1), :] = cols[pl.ds(rows_at[tile, at], 1), :]
            return mask ^ lax.shift_left(jnp.int32(1), 31 - at), rank + 1

        start = (rows_at[tile, half], rank)
        return lax.while_loop(lambda carry: carry[0] != 0, one_row, start)[1]

    lax.fori_loop(0, rows_at.shape[0], one_tile, jnp.int32(0))
    pack_rows(out, sent, members)


def pack_rows(rows, sent, members):
    packed = [rows[pl.ds(8 * at, 8), :] for at in range(SENT // 8)]
    spare = lax.broadcasted_iota(jnp.int32, (8, LANES), 1) >= members
    for at in range((ROOM - SENT) // 8):
        tail = rows[pl.ds(SENT + 8 * at, 8), :]
        for half, shift in enumerate((members, 2 * members - LANES)):
            here = 2 * at + half
            packed[here] = jnp.where(spare, pltpu.roll(tail, shift, 1), packed[here])
    for who in range(sent.shape[0]):
        for at, block in enumerate(packed):
            sent[who, pl.ds(8 * at, 8), :] = block


def unpack_rows(sent, rows, members):
    split = LANES - members
    lane = lax.broadcasted_iota(jnp.int32, (8, LANES), 1)
    for who in range(sent.shape[0]):
        rows[pl.ds(who * ROOM, SENT), :] = sent[who]
        for at in range((ROOM - SENT) // 8):
            one = pltpu.roll(sent[who, pl.ds(16 * at, 8), :], split, 1)
            two = pltpu.roll(sent[who, pl.ds(16 * at + 8, 8), :], 2 * split, 1)
            rows[pl.ds(who * ROOM + SENT + 8 * at, 8), :] = jnp.where(lane < split, one, two)


def repack_kernel(members, held, out):
    pack_rows(held, out, members)


def place_kernel(n_tile, owner, source, ranks, rounds, count):
    for at in range(n_tile):
        count[at] = 0

    def body(step, most):
        for part in range(8):
            row = step * 8 + part
            who = owner[row]
            rank = count[who]
            count[who] = rank + 1
            ranks[row] = rank
            source[row] = jnp.where(rank < ROOM, who * ROOM + rank, n_tile * ROOM + row)
            most = jnp.maximum(most, rank)
        return most

    rounds[0] = lax.fori_loop(0, owner.shape[0] // 8, body, jnp.int32(0)) // ROOM + 1


def rest_kernel(members, at, owner, ranks, sent, before, late, got):
    unpack_rows(sent, got, members)
    late[...] = before[...]

    def body(row, carry):
        rank = ranks[row] - at[0] * ROOM

        @pl.when((rank >= 0) & (rank < ROOM))
        def _():
            late[pl.ds(row, 1), :] = got[pl.ds(owner[row] * ROOM + rank, 1), :]

        return carry

    lax.fori_loop(0, late.shape[0], body, 0)


def take_rows(members, n_obs, part, batches, source, sent, late, outs, got):
    info = here()
    unpack_rows(sent, got, members)
    n_tile = sent.shape[0]
    got[pl.ds(n_tile * ROOM, late.shape[0]), :] = late[...]
    near = [lax.rem(info[2] - batch + n_obs, n_obs) for batch in batches]

    def body(step, carry):
        for half in range(2):
            who = step * 2 + half
            base = pl.multiple_of(step * 2 * part, 2 * part)
            for place, out in zip(near, outs):
                first = (who * n_obs + place) * part
                for row in range(part):
                    at = source[first + row]
                    out[pl.ds(base + half * part + row, 1), :] = got[pl.ds(at, 1), :]
        return carry

    lax.fori_loop(0, n_tile // 2, body, 0)


def first_kernel(members, n_obs, part, source, sent, late, meta, q, got, rows):
    take_rows(members, n_obs, part, [0], source, sent, late, [rows], got)
    q[pl.ds(0, members), :] = rows[...].T[:members]
    q[pl.ds(members, 8), :] = meta[...]


def others_kernel(members, n_obs, part, source, sent, late, *refs):
    take_rows(
        members, n_obs, part, range(1, n_obs), source, sent, late, refs[:-1], refs[-1]
    )


def weights(block, members):
    x = block[:members]
    mean = jnp.sum(x, axis=0, keepdims=True) / members
    pa = x - mean
    value = block[members + VALUE : members + VALUE + 1]
    var = block[members + VAR : members + VAR + 1]
    places = block[members + TILE : members + TILE + 1]
    total_var = jnp.sum(pa * pa, axis=0, keepdims=True) / (members - 1) + var
    alpha = 1.0 / (1.0 + jnp.sqrt(var / total_var))
    weight_a = alpha / total_var
    weight_d = (value - mean) / total_var
    left = (weight_d - weight_a * pa) / (members - 1)
    return pa, left, places


def add_block(acc, rows_x, pa3, left2, places, own_places):
    members = left2.shape[0] // 2
    high, low = halves(taper(own_places, places) * nn_dot(rows_x, pa3))
    return acc[0] + nt_dot(high, left2), acc[1] + nt_dot(low, left2[:members])


def zero_acc(n, members):
    return jnp.zeros((n, 2 * members), F32), jnp.zeros((n, members), F32)


def summed(acc):
    members = acc[1].shape[1]
    return acc[0][:, :members] + acc[0][:, members:] + acc[1]


def weigh(blocks, at, members, pa3_out, left_out, place_out):
    pa, left, places = weights(blocks[at], members)
    cols = pl.ds(at * WIDTH, WIDTH)
    pa3 = stacked(pa)
    pa3_out[:, cols] = pa3
    left_out[:, cols] = left
    place_out[:, cols] = places
    return pa3, left, places


def add_blocks(members, acc, blocks, xt, meta, outs):
    rows_x = side(xt[:, :members])
    own_places = meta[...].T[:, TILE : TILE + 1]
    for at in range(blocks.shape[0]):
        pa3, left, places = weigh(blocks, at, members, *outs)
        left2 = jnp.concatenate(halves(left), axis=0)
        acc = add_block(acc, rows_x, pa3, left2, places, own_places)
    return acc


def half_kernel(members, blocks, xt_ref, meta, high, low, *outs):
    acc = zero_acc(WIDTH, members)
    high[...], low[...] = add_blocks(members, acc, blocks, xt_ref[...], meta, outs)


def next_kernel(members, blocks, xt_ref, meta, high, low, q_out, *outs):
    xt = xt_ref[...]
    acc = add_blocks(members, (high[...], low[...]), blocks, xt, meta, outs)
    pad = jnp.zeros((WIDTH, LANES - members), F32)
    new = xt + jnp.concatenate([summed(acc), pad], axis=1)
    q_out[pl.ds(0, members), :] = new.T[:members]
    q_out[pl.ds(members, 8), :] = meta[...]


def add_gram(tiles, start, count, parts, gram, total):
    high_sum, low_sum = gram
    members = low_sum.shape[1]
    for pa3_ref, left_ref, place_ref in parts:
        for at in range(pa3_ref.shape[1] // WIDTH):
            cols = pl.ds(at * WIDTH, WIDTH)
            left = left_ref[pl.ds(start, count), cols]
            places = place_ref[:, cols]
            scaled = [left * taper(t.astype(F32) * (2.0 / total), places) for t in tiles]
            high, low = halves(jnp.concatenate(scaled, axis=0))
            pa3 = pa3_ref[:, cols]
            high_sum += nt_dot(high, pa3[members:])
            low_sum += nt_dot(low, pa3[:members])
    return high_sum, low_sum


def own_gram(members, tpd, info, parts, gram, total):
    start = pl.multiple_of(info[1] * (members // 2), 8)
    tiles = [info[0] + tile for tile in range(tpd)]
    return add_gram(tiles, start, members // 2, parts, gram, total)


def tiles_kernel(m_dev, tpd, own, other, tiles):
    info = here()
    core = info[1]
    n_half = tpd // 2
    for at in range(n_half):
        for part in range(own.shape[0] // (m_dev * tpd)):
            first = part * m_dev * tpd + at
            low, high = (pl.ds(first + n, m_dev, stride=tpd) for n in (0, n_half))
            a = jnp.where(core == 0, own[low, :], own[high, :])
            b = jnp.where(core == 0, other[low, :], other[high, :])
            whole = [jnp.where(core == 0, a, b), jnp.where(core == 0, b, a)]
            tiles[at, :, pl.ds(part * LANES, LANES)] = jnp.concatenate(whole, axis=0)


def later_kernel(members, total, n_later, n_state, *refs):
    info = here(total)
    refs = list(refs)
    take = lambda n: [refs.pop(0) for _ in range(n)]
    parts = [take(3), take(3)] if n_later else []
    xts, metas = take(n_later), take(n_later)
    batches = [[take(3), take(3)] for _ in range(n_state)]
    state = take(1)[0] if n_state else None
    for xt_ref, meta in zip(xts, metas):
        xt = xt_ref[...]
        rows_x = side(xt[:, :members])
        own_places = meta[...].T[:, TILE : TILE + 1]
        acc = zero_acc(WIDTH, members)
        for pa3_ref, left_ref, place_ref in parts:
            for at in range(pa3_ref.shape[1] // WIDTH):
                cols = pl.ds(at * WIDTH, WIDTH)
                left2 = jnp.concatenate(halves(left_ref[:, cols]), axis=0)
                acc = add_block(
                    acc, rows_x, pa3_ref[:, cols], left2, place_ref[:, cols], own_places
                )
        pad = jnp.zeros((WIDTH, LANES - members), F32)
        take(1)[0][...] = xt + jnp.concatenate([summed(acc), pad], axis=1)
    for which, sets in enumerate(batches):
        new = refs[0]
        n_tile = new.shape[0]
        tiles = [info[0] + info[1] * n_tile + at for at in range(n_tile)]
        gram = add_gram(tiles, 0, members, sets, zero_acc(n_tile * members, members), total)
        gram = side(summed(gram))
        for at in range(n_tile):
            whole = (new if which else state)[at]
            new[at] = whole + nn_dot(gram[at * members : (at + 1) * members], stacked(whole))


def gram_kernel(members, total, tpd, blocks, high, low, *parts):
    info = here(total)
    for at in range(blocks.shape[0]):
        weigh(blocks, at, members, *parts)
    gram = zero_acc(tpd * members // 2, members)
    high[...], low[...] = own_gram(members, tpd, info, [parts], gram, total)


def last_kernel(members, total, tpd, blocks, high, low, mine, other, out, new, *parts):
    info = here(total)
    for at in range(blocks.shape[0]):
        weigh(blocks, at, members, *parts)
    gram = own_gram(members, tpd, info, [parts], (high[...], low[...]), total)
    gram = side(summed(gram))
    m_dev, core = members // 2, info[1]
    n_half = mine.shape[0]
    for tile in range(tpd):
        at = tile % n_half
        whole = jnp.where(core == tile // n_half, mine[at], other[at])
        got = jnp.where(core == 0, whole[:m_dev], whole[m_dev:])
        got = got + nn_dot(gram[tile * m_dev : (tile + 1) * m_dev], stacked(whole))
        for part in range(got.shape[1] // LANES):
            row = pl.ds(part * m_dev * tpd + tile, m_dev, stride=tpd)
            new[row, :] = got[:, part * LANES : (part + 1) * LANES]
    rows = out.shape[0]
    for part in range(new.shape[0] // rows):
        out[:, pl.ds(part * LANES, LANES)] = new[pl.ds(part * rows, rows), :]


def vmem(n):
    return [pl.BlockSpec(memory_space=pltpu.VMEM)] * n


def smem(n):
    return [pl.BlockSpec(memory_space=pltpu.SMEM)] * n


def out_f32(*shape):
    return jax.ShapeDtypeStruct(shape, F32)


def ring(n, shift):
    return [(i, (i + shift) % n) for i in range(n)]


def call(kernel, name, n_smem, n_vmem, outs, flops, scratch=(), out_specs=None):
    return pl.pallas_call(
        kernel,
        out_shape=outs,
        in_specs=smem(n_smem) + vmem(n_vmem),
        out_specs=out_specs or (vmem(len(outs)) if isinstance(outs, list) else vmem(1)[0]),
        scratch_shapes=list(scratch),
        compiler_params=pltpu.CompilerParams(vmem_limit_bytes=24 * MIB),
        cost_estimate=pl.CostEstimate(flops=flops, bytes_accessed=4 * MIB, transcendentals=0),
        name=name,
    )


def per_device(ensemble, obs_cell, obs_value, obs_var):
    m_dev, tpd, points = ensemble.shape
    n_tile = lax.axis_size("tile")
    n_obs = lax.axis_size("obs")
    members = 2 * m_dev
    per_dev = obs_cell.shape[1]
    half = per_dev // 2
    part = half // n_obs
    batch_obs = per_dev * n_tile
    height = members + 8
    total = tpd * n_tile * n_obs
    slab_cells = tpd * points
    tile_at, obs_at, core = (lax.axis_index(a) for a in ("tile", "obs", "mem"))
    swap = functools.partial(lax.ppermute, axis_name="mem", perm=[(0, 1), (1, 0)])

    def shifted(x):
        return [x] + [lax.ppermute(x, "obs", ring(n_obs, k)) for k in range(1, n_obs)]

    def own_half(x):
        return lax.dynamic_slice(x, (0, core * half), (1, half))

    kind = lax.broadcasted_iota(jnp.int32, (4, half), 0)
    packed = jnp.where(kind == 1, own_half(obs_value), own_half(obs_var))
    packed = jnp.where(kind == 0, own_half(obs_cell).astype(F32), packed)
    near = shifted(packed)
    flat = (m_dev * tpd * points // LANES + 8, LANES)
    split = call(split_kernel, "split", 0, 1, out_f32(*flat), 10**6)
    state = split(ensemble.reshape(m_dev * tpd, points))
    chunks = shifted(state)
    others = [swap(chunk) for chunk in chunks]
    mix = functools.partial(mix_kernel, part)
    sent = call(mix, "mix", 0, n_obs, out_f32(n_tile, 1, 4 * half), 10**10)(*near)
    lists = lax.all_to_all(sent, "tile", 0, 0)
    n_rows = n_tile * half
    found = call(
        functools.partial(find_kernel, n_obs, slab_cells, half),
        "find",
        0,
        1,
        jax.ShapeDtypeStruct((n_tile, LANES), jnp.int32),
        10**10,
    )(lists)
    most_sends = -(-n_rows // ROOM)
    first, held = call(
        functools.partial(pick_kernel, n_obs, m_dev, tpd, half),
        "pick",
        1,
        2 * n_obs,
        [out_f32(n_tile, SENT, LANES), out_f32(most_sends * ROOM, LANES)],
        10**9,
        [
            pltpu.VMEM((n_obs * slab_cells, LANES), F32),
        ],
    )(found, *chunks, *others)
    first, lists = lax.optimization_barrier((first, lists))
    cells = lists[:, 0, :half].reshape(n_rows).astype(jnp.int32)
    owner = cells // (slab_cells * n_obs)
    ints = [jax.ShapeDtypeStruct((n,), jnp.int32) for n in (n_rows, n_rows, 1)]
    source, ranks, rounds = call(
        functools.partial(place_kernel, n_tile),
        "place",
        1,
        0,
        ints,
        10**9,
        [pltpu.SMEM((n_tile,), jnp.int32)],
        smem(3),
    )(owner)
    lists = jnp.transpose(lists.reshape(n_tile, 4, n_obs, part), (2, 1, 0, 3))
    lists = lists.reshape(n_obs, 4, WIDTH)
    metas = []
    for batch in range(n_obs):
        at = (obs_at - batch + n_obs) % n_obs
        one = lax.dynamic_slice(lists, (at, 0, 0), (1, 4, WIDTH))[0]
        place = (one[:1].astype(jnp.int32) // points).astype(F32) * (2.0 / total)
        metas.append(jnp.concatenate([one[1:3], place, jnp.zeros((5, WIDTH), F32)], axis=0))

    space = [pltpu.VMEM((n_tile * ROOM + n_rows, LANES), F32)]
    got = lax.all_to_all(first, "tile", 0, 0)

    def again(at, late):
        more = lax.dynamic_slice(held, (at * ROOM, 0), (ROOM, LANES))
        repack = functools.partial(repack_kernel, members)
        more = call(repack, "repack", 0, 1, out_f32(n_tile, SENT, LANES), 10**6)(more)
        got = lax.all_to_all(more, "tile", 0, 0)
        rest = functools.partial(rest_kernel, members)
        return call(rest, "rest", 3, 2, out_f32(n_rows, LANES), 10**8, space)(
            at.reshape(1), owner, ranks, got, late
        )

    got, late = lax.optimization_barrier((got, jnp.zeros((n_rows, LANES), F32)))
    late = lax.fori_loop(jnp.int32(1), rounds[0], again, late)
    q = call(
        functools.partial(first_kernel, members, n_obs, part),
        "first",
        1,
        3,
        out_f32(height, WIDTH),
        10**8,
        space + [pltpu.VMEM((WIDTH, LANES), F32)],
    )(source, got, late, metas[0])
    xts = call(
        functools.partial(others_kernel, members, n_obs, part),
        "others",
        1,
        2,
        [out_f32(WIDTH, LANES)] * (n_obs - 1),
        8 * 10**9,
        space,
    )(source, got, late)
    metas = metas[1:]
    own4 = jnp.stack(shifted(q))
    tiles = call(
        functools.partial(tiles_kernel, m_dev, tpd),
        "tiles",
        0,
        2,
        out_f32(tpd // 2, members, points),
        10**7,
    )(state, others[0])
    own4, xts, tiles = lax.optimization_barrier((own4, xts, tiles))
    oth4 = swap(own4)


    n_half = batch_obs // 2
    weighed = [
        jax.ShapeDtypeStruct((3 * members, n_half), BF16),
        out_f32(members, n_half),
        out_f32(1, n_half),
    ]
    space = [pltpu.VMEM(x.shape, x.dtype) for x in weighed]
    rows = tpd * m_dev
    parts = {}
    for batch in range(n_obs - 1):
        xt, xts, meta, metas = xts[0], xts[1:], metas[0], metas[1:]
        sums = [out_f32(WIDTH, 2 * members), out_f32(WIDTH, members)]
        high, low, *part_a = call(
            functools.partial(half_kernel, members), f"half{batch}", 0, 3, sums + weighed, 10**9
        )(own4, xt, meta)
        q, *part_b = call(
            functools.partial(next_kernel, members),
            f"next{batch}",
            0,
            5,
            [out_f32(height, WIDTH)] + weighed,
            10**9,
        )(oth4, xt, meta, high, low)
        own4 = jnp.stack(shifted(q))
        parts[batch] = part_a + part_b
        due = [[], [0], [1, 2]][batch]
        if xts:
            work = parts[batch] + list(xts) + metas
        else:
            work = []
        work += sum([parts[at] for at in due], []) + ([tiles] if due else [])
        outs = [out_f32(WIDTH, LANES)] * len(xts) + [out_f32(*tiles.shape)] * bool(due)
        done = call(
            functools.partial(later_kernel, members, total, len(xts), len(due)),
            f"later{batch}",
            0,
            len(work),
            outs,
            8 * 10**9,
        )(*work)
        own4, done = lax.optimization_barrier((own4, done))
        xts, tiles = list(done[: len(xts)]), done[-1] if due else tiles
        oth4 = swap(own4)
    other = swap(tiles)
    high, low = call(
        functools.partial(gram_kernel, members, total, tpd),
        "gram",
        0,
        1,
        [out_f32(rows, 2 * members), out_f32(rows, members)],
        2 * 10**9,
        space,
    )(own4)
    state = call(
        functools.partial(last_kernel, members, total, tpd),
        "last",
        0,
        5,
        out_f32(m_dev * tpd, points),
        2 * 10**9,
        [pltpu.VMEM(state.shape, F32)] + space,
    )(oth4, high, low, tiles, other)
    return state.reshape(m_dev, tpd, points)


def solution(mesh):
    return jax.shard_map(
        per_device,
        mesh=mesh,
        in_specs=(
            P("mem", ("tile", "obs"), None),
            P("obs", "tile"),
            P("obs", "tile"),
            P("obs", "tile"),
        ),
        out_specs=P("mem", ("tile", "obs"), None),
        check_vma=False,
    )
```
